128 devices in a mesh: section: 8 (over x, y_lo), fsdp: 16 (over y_hi, z, core).
Axes of the slice: x: 4, y: 4 (y_hi: 2, y_lo: 2; y = y_hi * 2 + y_lo), z: 4, core: 2. Of those that a mesh axis runs over, the one named last changes fastest.
Arguments:
- saved_inputs: bfloat16 [8, 2, 4096, 2048], P('section', None, 'fsdp'), may hold values from -600 to 600
- saved_queries: bfloat16 [8, 2, 4096, 1024], P('section', None, 'fsdp'), may hold values from -300 to 300
- saved_keys: bfloat16 [8, 2, 4096, 256], P('section', None, 'fsdp'), may hold values from -6 to 6
- saved_values: bfloat16 [8, 2, 4096, 256], P('section', None, 'fsdp'), may hold values from -6 to 6
- cotangent: bfloat16 [2, 4096, 2048], P(None, 'fsdp'), may hold values from -6 to 6
- norm_gain: bfloat16 [8, 2048], P('section'), may hold values from 0.099609375 to 1.8984375
- query_weight: bfloat16 [8, 2048, 1024], P('section', 'fsdp'), may hold values from -0.125 to 0.125
- key_weight: bfloat16 [8, 2048, 256], P('section', 'fsdp'), may hold values from -0.125 to 0.125
- value_weight: bfloat16 [8, 2048, 256], P('section', 'fsdp'), may hold values from -0.125 to 0.125
- output_weight: bfloat16 [8, 2048, 1024], P('section', 'fsdp'), may hold values from -0.1875 to 0.1875
Outputs:
- act_grads: bfloat16 [8, 2, 4096, 2048], P('section', None, 'fsdp')
- grad_query: bfloat16 [8, 2048, 1024], P('section', 'fsdp')
- grad_key: bfloat16 [8, 2048, 256], P('section', 'fsdp')
- grad_value: bfloat16 [8, 2048, 256], P('section', 'fsdp')
- grad_output: bfloat16 [8, 2048, 1024], P('section', 'fsdp')
The draws below stay inside these ranges and needn't reach their ends.
All inputs are finite; a program needn't handle non-finite values.
Results may differ from the reference program's by a relative error of at most 0.024.
Values may be sent and summed in bfloat16 or wider, within the bound.
No kernel may reach another device: no remote copies, remote signals or barrier semaphores. Data moves between devices by JAX's collectives and lax.ppermute only.
A program may use at most 128 MiB of HBM per device.

```python
import math
import jax
import jax.numpy as jnp
from jax import lax

D = 2048
HEADS = 16
KVH = 4
HD = 64
SEQ = 256
MICRO = 2
LAYERS = 8
TOKENS = 4096
QD = 1024
KVD = 256
QKV = 1536


def shared_keys(key):
    base = jax.random.normal(jax.random.fold_in(key, 101), (LAYERS, MICRO, TOKENS, KVD), jnp.float32)
    return jnp.clip(base, -6.0, 6.0)


def draw_saved_inputs(key, part):
    key = jax.random.fold_in(key, 7)
    row_key, col_key, noise_key = jax.random.split(key, 3)
    row_scale = jnp.exp(jax.random.uniform(row_key, (LAYERS, MICRO, TOKENS, 1), jnp.float32, 0.0, math.log(10.0)))
    col_scale = jnp.exp(jax.random.uniform(col_key, (LAYERS, 1, 1, D), jnp.float32, 0.0, math.log(10.0)))
    noise = jnp.clip(jax.random.normal(noise_key, (LAYERS, MICRO, TOKENS, D), jnp.float32), -6.0, 6.0)
    return (noise * row_scale * col_scale).astype(jnp.bfloat16)


def draw_saved_keys(key, part):
    base = shared_keys(key)
    return base.astype(jnp.bfloat16)


def draw_saved_queries(key, part):
    key = jax.random.fold_in(key, 5)
    queries = jnp.clip(jax.random.normal(key, (LAYERS, MICRO, TOKENS, QD), jnp.float32), -6.0, 6.0)
    return queries.astype(jnp.bfloat16)


def level_of(key, shape, cuts, smallest, high):
    level = 1.0
    for position, shards_of in cuts:
        steps = jax.random.uniform(jax.random.fold_in(jax.random.fold_in(key, 6), position), (shards_of,), jnp.float32, smallest / len(cuts), high / len(cuts))
        level = level * jnp.repeat(jnp.exp(steps), shape[position] // shards_of).reshape((-1,) + (1,) * (len(shape) - 1 - position))
    return level


def centred(key, shape, scale, most, cuts=(), held_as=jnp.bfloat16):
    level = level_of(key, shape, cuts, -0.22, 0.18) if cuts else 1.0
    values = jax.random.normal(key, shape, jnp.float32) * scale * level
    return jnp.minimum(jnp.maximum(values, -most), most).astype(held_as)


def setup_inputs(seed: int = 0) -> dict:
    splits = jax.random.split(jax.random.key(seed), 11)
    saved_inputs = draw_saved_inputs(jax.random.fold_in(splits[10], 71), 0)
    saved_queries = draw_saved_queries(jax.random.fold_in(splits[10], 71), 0)
    saved_keys = draw_saved_keys(jax.random.fold_in(splits[10], 71), 0)
    saved_values = centred(splits[3], (LAYERS, MICRO, TOKENS, KVD), 1.0, 6.0, ((0, 8), (2, 16)))
    cotangent = centred(splits[4], (MICRO, TOKENS, D), 1.0, 6.0, ((1, 16),))
    norm_gain = jnp.clip(1.0 + 0.18 * jax.random.normal(splits[5], (LAYERS, D), jnp.float32), 0.099609375, 1.8984375).astype(jnp.bfloat16)
    query_weight = centred(splits[6], (LAYERS, D, QD), D ** -0.5, 0.125, ((0, 8), (1, 16)))
    key_weight = centred(splits[7], (LAYERS, D, KVD), D ** -0.5, 0.125, ((0, 8), (1, 16)))
    value_weight = centred(splits[8], (LAYERS, D, KVD), D ** -0.5, 0.125, ((0, 8), (1, 16)))
    output_weight = centred(splits[9], (LAYERS, D, QD), QD ** -0.5, 0.1875, ((0, 8), (1, 16)))
    return {"saved_inputs": saved_inputs, "saved_queries": saved_queries, "saved_keys": saved_keys, "saved_values": saved_values, "cotangent": cotangent, "norm_gain": norm_gain, "query_weight": query_weight, "key_weight": key_weight, "value_weight": value_weight, "output_weight": output_weight}


norm_eps = 1e-05
rotary_base = 500000.0
masked_score = -1e+30

def rotary_tables(length, head_size):
    half_size = head_size // 2
    inverse = jnp.exp(-(2.0 * jnp.arange(half_size, dtype=jnp.float32) / head_size) * math.log(rotary_base))
    angles = jnp.arange(length, dtype=jnp.float32)[:, None] * inverse[None, :]
    return (jnp.cos(angles), jnp.sin(angles))

def rotate_back(grad_rows, cosine_table, sine_table):
    half_size = grad_rows.shape[-1] // 2
    front_half = grad_rows[..., :half_size]
    back_half = grad_rows[..., half_size:]
    cos_rows = cosine_table[:, None, :]
    sin_rows = sine_table[:, None, :]
    return jnp.concatenate([front_half * cos_rows + back_half * sin_rows, back_half * cos_rows - front_half * sin_rows], axis=-1)

def section_backward(inputs, queries, keys, values, upstream, in_full, out_full, gain_row, cosine_table, sine_table):
    sequences = inputs.shape[0] // SEQ
    groups = HEADS // KVH
    scaling = 1.0 / math.sqrt(HD)
    inputs_f = inputs.astype(jnp.float32)
    scale_inv = lax.rsqrt(lax.optimization_barrier(jnp.mean(inputs_f * inputs_f, axis=-1, keepdims=True)) + norm_eps)
    unit_rows = inputs_f * scale_inv
    gain_vec = gain_row.astype(jnp.float32)
    normed = (unit_rows * gain_vec).astype(jnp.bfloat16)
    query_grid = queries.reshape(sequences, SEQ, KVH, groups, HD).astype(jnp.float32)
    key_grid = keys.reshape(sequences, SEQ, KVH, HD).astype(jnp.float32)
    value_grid = values.reshape(sequences, SEQ, KVH, HD).astype(jnp.float32)
    scores = jnp.einsum('ntkgd,nskd->nkgts', query_grid, key_grid) * scaling
    causal = jnp.arange(SEQ)[:, None] >= jnp.arange(SEQ)[None, :]
    scores = jnp.where(causal, scores, masked_score)
    row_peak = lax.optimization_barrier(jnp.max(scores, axis=-1, keepdims=True))
    weights = jnp.exp(scores - row_peak)
    attn_probs = lax.optimization_barrier((weights / lax.optimization_barrier(jnp.sum(weights, axis=-1, keepdims=True))).astype(jnp.bfloat16)).astype(jnp.float32)
    attn_out = jnp.einsum('nkgts,nskd->ntkgd', attn_probs, value_grid).astype(jnp.bfloat16).reshape(-1, QD)
    d_attn = jnp.dot(upstream, out_full, preferred_element_type=jnp.float32).astype(jnp.bfloat16)
    attn_grid = lax.optimization_barrier(d_attn).reshape(sequences, SEQ, KVH, groups, HD).astype(jnp.float32)
    d_probs = jnp.einsum('ntkgd,nskd->nkgts', attn_grid, value_grid)
    row_inner = lax.optimization_barrier(jnp.sum(attn_probs * d_probs, axis=-1, keepdims=True))
    d_scores = lax.optimization_barrier((attn_probs * (d_probs - row_inner) * scaling).astype(jnp.bfloat16)).astype(jnp.float32)
    d_query = jnp.einsum('nkgts,nskd->ntkgd', d_scores, key_grid)
    d_key = jnp.einsum('nkgts,ntkgd->nskd', d_scores, query_grid)
    d_value = jnp.einsum('nkgts,ntkgd->nskd', attn_probs, attn_grid)
    d_query = rotate_back(d_query.reshape(sequences, SEQ, HEADS, HD), cosine_table, sine_table)
    d_key = rotate_back(d_key, cosine_table, sine_table)
    grad_qkv = jnp.concatenate([d_query.reshape(-1, QD), d_key.reshape(-1, KVD), d_value.reshape(-1, KVD)], axis=1).astype(jnp.bfloat16)
    d_normed = jnp.dot(grad_qkv, in_full.T, preferred_element_type=jnp.float32)
    scaled = d_normed * gain_vec
    d_inputs = scale_inv * (scaled - unit_rows * lax.optimization_barrier(jnp.mean(scaled * unit_rows, axis=-1, keepdims=True)))
    grad_in = (upstream.astype(jnp.float32) + d_inputs).astype(jnp.bfloat16)
    return (grad_in, normed, grad_qkv, attn_out)

def per_sequence(stacked):
    micro_count = stacked.shape[0]
    sequences = stacked.shape[1] // SEQ
    return stacked.reshape(micro_count, sequences, SEQ, -1).transpose(1, 0, 2, 3).reshape(sequences, micro_count * SEQ, -1)

def weight_grads(normed_all, qkv_all, attn_all, upstream_all):
    blocks = (per_sequence(normed_all), per_sequence(qkv_all), per_sequence(attn_all), per_sequence(upstream_all))

    def add_block(running, seq_block):
        normed_rows, qkv_rows, attn_rows, upstream_rows = seq_block
        in_term = jnp.dot(normed_rows.T, qkv_rows, preferred_element_type=jnp.float32)
        out_term = jnp.dot(upstream_rows.T, attn_rows, preferred_element_type=jnp.float32)
        rounded = lax.optimization_barrier(jnp.concatenate([in_term, out_term], axis=1).astype(jnp.bfloat16))
        return (running + rounded.astype(jnp.float32), None)
    initial = jnp.zeros((D, QKV + QD), jnp.float32)
    running, leftover = lax.scan(add_block, initial, blocks)
    return running.astype(jnp.bfloat16)

def reference(saved_inputs, saved_queries, saved_keys, saved_values, cotangent, norm_gain, query_weight, key_weight, value_weight, output_weight):
    cosine_table, sine_table = rotary_tables(SEQ, HD)
    upstream = [cotangent[micro_index] for micro_index in range(MICRO)]
    act_layers = [None] * LAYERS
    query_layers = [None] * LAYERS
    key_layers = [None] * LAYERS
    value_layers = [None] * LAYERS
    output_layers = [None] * LAYERS
    for layer_index in range(LAYERS - 1, -1, -1):
        in_full = jnp.concatenate([query_weight[layer_index], key_weight[layer_index], value_weight[layer_index]], axis=1)
        results = [section_backward(saved_inputs[layer_index, micro_index], saved_queries[layer_index, micro_index], saved_keys[layer_index, micro_index], saved_values[layer_index, micro_index], upstream[micro_index], in_full, output_weight[layer_index], norm_gain[layer_index], cosine_table, sine_table) for micro_index in range(MICRO)]
        act_layers[layer_index] = jnp.stack([result[0] for result in results])
        summed = weight_grads(jnp.stack([result[1] for result in results]), jnp.stack([result[2] for result in results]), jnp.stack([result[3] for result in results]), jnp.stack(upstream))
        query_layers[layer_index] = summed[:, :QD]
        key_layers[layer_index] = summed[:, QD:QD + KVD]
        value_layers[layer_index] = summed[:, QD + KVD:QKV]
        output_layers[layer_index] = summed[:, QKV:]
        upstream = [result[0] for result in results]
    return (jnp.stack(act_layers), jnp.stack(query_layers), jnp.stack(key_layers), jnp.stack(value_layers), jnp.stack(output_layers))
```

```python
import functools
import math

import jax
import jax.numpy as jnp
from jax import lax
from jax.experimental import pallas as pl
from jax.experimental.pallas import tpu as pltpu
from jax.sharding import PartitionSpec as P

HEADS = 16
KVH = 4
HD = 64
ROWS = 64
norm_eps = 1e-05
rotary_base = 500000.0
masked_score = -1e30
F32 = jnp.float32
BF16 = jnp.bfloat16


def passed_down(block):
    size = lax.axis_size("section")
    return lax.ppermute(block, "section", [(i, i - 1) for i in range(1, size)])


def rotary_tables(length):
    half = HD // 2
    inverse = jnp.exp(-(2.0 * jnp.arange(half, dtype=F32) / HD) * math.log(rotary_base))
    angles = jnp.arange(length, dtype=F32)[:, None] * inverse[None, :]
    return jnp.cos(angles), jnp.sin(angles)


def low_lanes(shape):
    return lax.broadcasted_iota(jnp.int32, shape, 1) < HD


def forward_kernel(x_ref, q_ref, kbd_ref, vdup_ref, gain_ref, normed_ref, p_ref, attn_ref, qt_ref):
    chunk = pl.program_id(1)
    x = x_ref[0].astype(F32)
    inv = lax.rsqrt(jnp.mean(x * x, axis=-1, keepdims=True) + norm_eps)
    normed_ref[0] = (x * inv * gain_ref[...].astype(F32)).astype(BF16)
    length = vdup_ref.shape[2]
    shape = (2 * ROWS, length)
    row = lax.broadcasted_iota(jnp.int32, shape, 0)
    row = jnp.where(row >= ROWS, row - ROWS, row) + chunk * ROWS
    keep = row >= lax.broadcasted_iota(jnp.int32, shape, 1)
    low = low_lanes((ROWS, 128))
    for g in range(KVH):
        pairs = jnp.concatenate([q_ref[0, :, g * 256 + j * 128 : g * 256 + (j + 1) * 128] for j in range(2)], axis=0)
        qt_ref[0, 0, g] = pairs.astype(F32).T.astype(BF16)
        scores = jnp.dot(pairs, kbd_ref[0, g], preferred_element_type=F32) * (1.0 / math.sqrt(HD))
        halves = []
        for e in range(2):
            part = jnp.where(keep, scores[:, e * length : (e + 1) * length], masked_score)
            weights = jnp.exp(part - jnp.max(part, axis=-1, keepdims=True))
            halves.append((weights / jnp.sum(weights, axis=-1, keepdims=True)).astype(BF16))
            p_ref[0, 0, g * 2 * ROWS : (g + 1) * 2 * ROWS, e * length : (e + 1) * length] = halves[e]
        out = jnp.dot(jnp.concatenate(halves, axis=0), vdup_ref[0, g], preferred_element_type=F32)
        for j in range(2):
            even = out[j * ROWS : (j + 1) * ROWS]
            odd = out[(2 + j) * ROWS : (3 + j) * ROWS]
            attn_ref[0, :, g * 256 + j * 128 : g * 256 + (j + 1) * 128] = jnp.where(low, even, odd).astype(BF16)


def forward_parts(x, q, kbd, vdup, gain):
    micro, length, width = x.shape
    chunks = length // ROWS
    return pl.pallas_call(
        forward_kernel,
        grid=(micro, chunks),
        in_specs=[
            pl.BlockSpec((1, ROWS, width), lambda m, c: (m, c, 0)),
            pl.BlockSpec((1, ROWS, HEADS * HD), lambda m, c: (m, c, 0)),
            pl.BlockSpec((1, KVH, 128, 2 * length), lambda m, c: (m, 0, 0, 0)),
            pl.BlockSpec((1, KVH, length, 128), lambda m, c: (m, 0, 0, 0)),
            pl.BlockSpec((1, width), lambda m, c: (0, 0)),
        ],
        out_specs=[
            pl.BlockSpec((1, ROWS, width), lambda m, c: (m, c, 0)),
            pl.BlockSpec((1, 1, KVH * 2 * ROWS, 2 * length), lambda m, c: (m, c, 0, 0)),
            pl.BlockSpec((1, ROWS, HEADS * HD), lambda m, c: (m, c, 0)),
            pl.BlockSpec((1, 1, KVH, 128, 2 * ROWS), lambda m, c: (m, c, 0, 0, 0)),
        ],
        out_shape=[
            jax.ShapeDtypeStruct((micro, length, width), BF16),
            jax.ShapeDtypeStruct((micro, chunks, KVH * 2 * ROWS, 2 * length), BF16),
            jax.ShapeDtypeStruct((micro, length, HEADS * HD), BF16),
            jax.ShapeDtypeStruct((micro, chunks, KVH, 128, 2 * ROWS), BF16),
        ],
        compiler_params=pltpu.CompilerParams(vmem_limit_bytes=24 << 20),
        name="forward_parts",
    )(x, q, kbd, vdup, gain)


def turn_kernel(
    micro, turn,
    place_ref, arrived_ref, cot_ref, x_any, p_any, qt_any, kcat_any, vbd_any, gain_ref, cs_any, ct_ref, st_ref,
    w_ref, acc_in, act_in, qkv_in, up_in,
    act_out, acc_any, act_any, qkv_any, up_any,
    up_ref, x_ref, p_ref, qt_ref, kcat_ref, vbd_ref, cs_ref, gq_ref, g_ref, acc_ref, sems, acc_sem, cot_sem, up_sem, qkv_sem, act_sem,
):
    chunk, active, first, fresh = [place_ref[4 * turn + i] for i in range(4)]
    rows = pl.ds(pl.multiple_of(chunk * ROWS, ROWS), ROWS)
    qd, kvd = HEADS * HD, KVH * HD
    qkv = qd + 2 * kvd
    width = up_ref.shape[1]
    length = ct_ref.shape[1]
    loads = [
        pltpu.make_async_copy(vbd_any.at[micro], vbd_ref, sems.at[0]),
        pltpu.make_async_copy(p_any.at[micro, chunk], p_ref, sems.at[1]),
        pltpu.make_async_copy(kcat_any.at[micro], kcat_ref, sems.at[2]),
        pltpu.make_async_copy(qt_any.at[micro, chunk], qt_ref, sems.at[3]),
        pltpu.make_async_copy(cs_any.at[rows], cs_ref, sems.at[4]),
        pltpu.make_async_copy(x_any.at[micro, rows], x_ref, sems.at[5]),
        pltpu.make_async_copy(acc_in, acc_ref, sems.at[6]),
    ]

    @pl.when(first == 1)
    def _():
        copy = pltpu.make_async_copy(cot_ref.at[micro, rows], up_ref, cot_sem)
        copy.start()
        copy.wait()

    @pl.when(first == 0)
    def _():
        up_ref[...] = arrived_ref[...]

    for load in loads:
        load.start()
    keep_up = pltpu.make_async_copy(up_ref, up_any.at[micro, rows], up_sem)

    @pl.when(active == 1)
    def _():
        keep_up.start()

    d_attn = [
        jnp.dot(up_ref[...], w_ref[:, qkv + g * 256 : qkv + (g + 1) * 256], preferred_element_type=F32)
        for g in range(KVH)
    ]
    for load in loads:
        load.wait()
    low = low_lanes((ROWS, 128))
    cs4 = jnp.concatenate([cs_ref[...]] * 4, axis=0)
    for g in range(KVH):
        pairs_f = jnp.concatenate([d_attn[g][:, :128], d_attn[g][:, 128:]], axis=0)
        pairs = pairs_f.astype(BF16)
        probs_b = p_ref[g * 2 * ROWS : (g + 1) * 2 * ROWS, :]
        probs = probs_b.astype(F32)
        d_probs = jnp.dot(pairs, vbd_ref[g], preferred_element_type=F32)
        inner = probs * d_probs
        scores = []
        for e in range(2):
            part = slice(e * length, (e + 1) * length)
            row_inner = jnp.sum(inner[:, part], axis=-1, keepdims=True)
            scores.append((probs[:, part] * (d_probs[:, part] - row_inner) * (1.0 / math.sqrt(HD))).astype(BF16))
        stacked = jnp.concatenate(scores, axis=0)
        turned = jnp.dot(stacked, kcat_ref[g], preferred_element_type=F32) * cs4
        turned = turned + pltpu.roll(turned, HD, 1)
        for j in range(2):
            even = turned[j * ROWS : (j + 1) * ROWS]
            odd = turned[(2 + j) * ROWS : (3 + j) * ROWS]
            gq_ref[:, g * 256 + j * 128 : g * 256 + (j + 1) * 128] = jnp.where(low, even, odd).astype(BF16)
        feats = slice(g * HD, (g + 1) * HD)
        vfeats = slice(kvd + g * HD, kvd + (g + 1) * HD)
        wide = jnp.concatenate(scores, axis=1)
        dk2 = jnp.dot(qt_ref[g], wide, preferred_element_type=F32)
        dk = dk2[:HD, :length] + dk2[HD:, length:]
        front, back = dk[: HD // 2], dk[HD // 2 :]
        dk = jnp.concatenate(
            [front * ct_ref[...] + back * st_ref[...], back * ct_ref[...] - front * st_ref[...]], axis=0
        )
        dv2 = jnp.dot(pairs.astype(F32).T.astype(BF16), probs_b, preferred_element_type=F32)
        dv = dv2[:HD, :length] + dv2[HD:, length:]
        acc_ref[feats] = jnp.where(fresh == 1, dk, acc_ref[feats] + dk)
        acc_ref[vfeats] = jnp.where(fresh == 1, dv, acc_ref[vfeats] + dv)
    keep_acc = pltpu.make_async_copy(acc_ref, acc_any, acc_sem)
    keep_acc.start()
    slab = acc_ref[:, pl.ds(pl.multiple_of((chunk // 2) * 128, 128), 128)].T
    done = jnp.where(chunk % 2 == 1, slab[ROWS:], slab[:ROWS])
    gq_ref[:, qd:] = done.astype(BF16)
    keep_qkv = pltpu.make_async_copy(gq_ref, qkv_any.at[micro, rows], qkv_sem)

    @pl.when(active == 1)
    def _():
        keep_qkv.start()

    x = x_ref[...].astype(F32)
    inv = lax.rsqrt(jnp.mean(x * x, axis=-1, keepdims=True) + norm_eps)
    total = jnp.zeros((ROWS, 256), F32)
    for n in range(width // 256):
        cols = slice(n * 256, (n + 1) * 256)
        d_normed = lax.dot_general(
            gq_ref[...], w_ref[cols, :qkv], (((1,), (1,)), ((), ())), preferred_element_type=F32
        )
        scaled = d_normed * gain_ref[:, cols].astype(F32)
        g_ref[:, cols] = scaled
        total = total + scaled * (x_ref[:, cols].astype(F32) * inv)
    mean = jnp.sum(total, axis=-1, keepdims=True) * (1.0 / width)
    for n in range(width // 256):
        cols = slice(n * 256, (n + 1) * 256)
        unit = x_ref[:, cols].astype(F32) * inv
        act_out[:, cols] = (up_ref[:, cols].astype(F32) + inv * (g_ref[:, cols] - unit * mean)).astype(BF16)
    keep_act = pltpu.make_async_copy(act_out, act_any.at[micro, rows], act_sem)

    keep_acc.wait()

    @pl.when(active == 1)
    def _():
        keep_act.start()
        keep_up.wait()
        keep_qkv.wait()
        keep_act.wait()


def turn_step(micro, turn, place, arrived, cot, x, p, qt, kcat, vbd, gain, cs, ct, st, w, acc, act, qkv, up):
    width = x.shape[-1]
    length = x.shape[1]
    any_spec = pl.BlockSpec(memory_space=pltpu.HBM)
    vmem = pl.BlockSpec(memory_space=pltpu.VMEM)
    w = pltpu.with_memory_space_constraint(w, pltpu.VMEM)
    acc = pltpu.with_memory_space_constraint(acc, pltpu.HBM)
    cot, x, p, qt, kcat, vbd, cs, act, qkv, up = [pltpu.with_memory_space_constraint(b, pltpu.HBM) for b in (cot, x, p, qt, kcat, vbd, cs, act, qkv, up)]
    like = lambda a: jax.ShapeDtypeStruct(a.shape, a.dtype)
    return pl.pallas_call(
        functools.partial(turn_kernel, micro, turn),
        in_specs=[
            pl.BlockSpec(memory_space=pltpu.SMEM), vmem, any_spec, any_spec, any_spec, any_spec, any_spec, any_spec,
            vmem, any_spec, vmem, vmem, vmem, any_spec, any_spec, any_spec, any_spec,
        ],
        out_specs=[vmem, any_spec, any_spec, any_spec, any_spec],
        out_shape=[jax.ShapeDtypeStruct((ROWS, width), BF16), pltpu.HBM(acc.shape, acc.dtype), pltpu.HBM(act.shape, act.dtype), pltpu.HBM(qkv.shape, qkv.dtype), pltpu.HBM(up.shape, up.dtype)],
        input_output_aliases={13: 1, 14: 2, 15: 3, 16: 4},
        scratch_shapes=[
            pltpu.VMEM((ROWS, width), BF16),
            pltpu.VMEM((ROWS, width), BF16),
            pltpu.VMEM(p.shape[2:], BF16),
            pltpu.VMEM(qt.shape[2:], BF16),
            pltpu.VMEM(kcat.shape[1:], BF16),
            pltpu.VMEM(vbd.shape[1:], BF16),
            pltpu.VMEM((ROWS, 128), F32),
            pltpu.VMEM((ROWS, qkv.shape[-1]), BF16),
            pltpu.VMEM((ROWS, width), F32),
            pltpu.VMEM(acc.shape, F32),
            pltpu.SemaphoreType.DMA((7,)),
            pltpu.SemaphoreType.DMA,
            pltpu.SemaphoreType.DMA,
            pltpu.SemaphoreType.DMA,
            pltpu.SemaphoreType.DMA,
            pltpu.SemaphoreType.DMA,
        ],
        compiler_params=pltpu.CompilerParams(vmem_limit_bytes=8 << 20),
        cost_estimate=pl.CostEstimate(flops=2 * ROWS * width * 2560 * 4, bytes_accessed=12 << 20, transcendentals=0),
        name="turn_step",
    )(place, arrived, cot, x, p, qt, kcat, vbd, gain, cs, ct, st, w, acc, act, qkv, up)


def weight_kernel(normed_ref, qkv_ref, up_ref, attn_ref, out_ref):
    dims = (((0,), (0,)), ((), ()))
    qkv = qkv_ref.shape[1]
    for start in range(0, qkv, 512):
        out_ref[:, start : start + 512] = lax.dot_general(
            normed_ref[...], qkv_ref[:, start : start + 512], dims, preferred_element_type=F32
        ).astype(BF16)
    for start in range(0, attn_ref.shape[1], 512):
        out_ref[:, qkv + start : qkv + start + 512] = lax.dot_general(
            up_ref[...], attn_ref[:, start : start + 512], dims, preferred_element_type=F32
        ).astype(BF16)


def weight_parts(normed, qkv, up, attn):
    tokens, width = normed.shape
    total = qkv.shape[1] + attn.shape[1]
    tile = 256
    return pl.pallas_call(
        weight_kernel,
        grid=(width // tile,),
        in_specs=[
            pl.BlockSpec((tokens, tile), lambda i: (0, i)),
            pl.BlockSpec(qkv.shape, lambda i: (0, 0)),
            pl.BlockSpec((tokens, tile), lambda i: (0, i)),
            pl.BlockSpec(attn.shape, lambda i: (0, 0)),
        ],
        out_specs=pl.BlockSpec((tile, total), lambda i: (i, 0)),
        out_shape=jax.ShapeDtypeStruct((width, total), BF16),
        compiler_params=pltpu.CompilerParams(vmem_limit_bytes=32 << 20),
        name="weight_parts",
    )(normed, qkv, up, attn)


def paired(blocks):
    turned = blocks.transpose(0, 2, 3, 1)
    zero = jnp.zeros_like(turned)
    return jnp.concatenate(
        [jnp.concatenate([turned, zero], axis=3), jnp.concatenate([zero, turned], axis=3)], axis=2
    )


def on_device(x, q, k, v, cot, gain, wq, wk, wv, wo):
    sections = lax.axis_size("section")
    me = lax.axis_index("section")
    x, q, k, v, gain = x[0], q[0], k[0], v[0], gain
    micro, length, width = x.shape
    chunks = length // ROWS
    shard = jnp.concatenate([wq[0], wk[0], wv[0], wo[0]], axis=1)
    w = lax.all_gather(shard, "fsdp", axis=0, tiled=True)
    kh = k.reshape(micro, length, KVH, HD)
    vh = v.reshape(micro, length, KVH, HD)
    kg = kh.transpose(0, 2, 1, 3)
    vg = vh.transpose(0, 2, 1, 3)
    swapped = jnp.concatenate([kg[..., HD // 2 :], kg[..., : HD // 2]], axis=-1)
    kcat = jnp.concatenate([kg, swapped], axis=-1)
    vdup = jnp.concatenate([vg, vg], axis=-1)
    cos, sin = rotary_tables(length)
    cs = jnp.concatenate([cos, cos, sin, -sin], axis=1)
    normed, p, attn, qt = forward_parts(x, q, paired(kh), vdup, gain)
    vbd = paired(vh)
    ct, st = cos.T, sin.T
    acc = [jnp.zeros((2 * KVH * HD, length), F32) for _ in range(micro)]
    act = jnp.zeros((micro, length, width), BF16)
    qkv = jnp.zeros((micro, length, (HEADS + 2 * KVH) * HD), BF16)
    up = jnp.zeros((micro, length, width), BF16)
    arrived = [jnp.zeros((ROWS, width), BF16) for _ in range(micro)]
    turns = sections - 1 + chunks
    step = jnp.arange(turns, dtype=jnp.int32) - (sections - 1 - me)
    place = jnp.stack(
        [
            chunks - 1 - jnp.clip(step, 0, chunks - 1),
            ((step >= 0) & (step < chunks)).astype(jnp.int32),
            jnp.broadcast_to((me == sections - 1).astype(jnp.int32), (turns,)),
            (step <= 0).astype(jnp.int32),
        ],
        axis=1,
    ).reshape(-1)
    for turn in range(turns):
        for m in range(micro):
            sent, acc[m], act, qkv, up = turn_step(
                m, turn, place, arrived[m], cot, x, p, qt, kcat, vbd, gain, cs, ct, st, w, acc[m], act, qkv, up
            )
            if turn < turns - 1:
                arrived[m] = passed_down(sent)
    parts = weight_parts(
        normed.reshape(micro * length, width),
        qkv.reshape(micro * length, -1),
        up.reshape(micro * length, width),
        attn.reshape(micro * length, -1),
    )
    summed = lax.psum_scatter(parts, "fsdp", scatter_dimension=0, tiled=True)
    qd, kvd = HEADS * HD, KVH * HD
    return (
        act[None],
        summed[None, :, :qd],
        summed[None, :, qd : qd + kvd],
        summed[None, :, qd + kvd : qd + 2 * kvd],
        summed[None, :, qd + 2 * kvd :],
    )


def solution(mesh):
    row = P("section", None, "fsdp", None)
    weight = P("section", "fsdp", None)
    return jax.shard_map(
        on_device,
        mesh=mesh,
        in_specs=(row, row, row, row, P(None, "fsdp", None), P("section", None), weight, weight, weight, weight),
        out_specs=(row, weight, weight, weight, weight),
        check_vma=False,
    )
```

```python
import functools
import math

import jax
import jax.numpy as jnp
from jax import lax
from jax.experimental import pallas as pl
from jax.experimental.pallas import tpu as pltpu
from jax.sharding import PartitionSpec as P

HEADS = 16
KVH = 4
HD = 64
ROWS = 64
norm_eps = 1e-05
rotary_base = 500000.0
masked_score = -1e30
F32 = jnp.float32
BF16 = jnp.bfloat16


def passed_down(block):
    size = lax.axis_size("section")
    return lax.ppermute(block, "section", [(i, i - 1) for i in range(1, size)])


def rotary_tables(length):
    half = HD // 2
    inverse = jnp.exp(-(2.0 * jnp.arange(half, dtype=F32) / HD) * math.log(rotary_base))
    angles = jnp.arange(length, dtype=F32)[:, None] * inverse[None, :]
    return jnp.cos(angles), jnp.sin(angles)


def low_lanes(shape):
    return lax.broadcasted_iota(jnp.int32, shape, 1) < HD


def forward_kernel(x_ref, q_ref, kbd_ref, vdup_ref, gain_ref, normed_ref, p_ref, attn_ref, qt_ref):
    chunk = pl.program_id(1)
    x = x_ref[0].astype(F32)
    inv = lax.rsqrt(jnp.mean(x * x, axis=-1, keepdims=True) + norm_eps)
    normed_ref[0] = (x * inv * gain_ref[...].astype(F32)).astype(BF16)
    length = vdup_ref.shape[2]
    shape = (2 * ROWS, length)
    row = lax.broadcasted_iota(jnp.int32, shape, 0)
    row = jnp.where(row >= ROWS, row - ROWS, row) + chunk * ROWS
    keep = row >= lax.broadcasted_iota(jnp.int32, shape, 1)
    low = low_lanes((ROWS, 128))
    for g in range(KVH):
        pairs = jnp.concatenate([q_ref[0, :, g * 256 + j * 128 : g * 256 + (j + 1) * 128] for j in range(2)], axis=0)
        qt_ref[0, 0, g] = pairs.astype(F32).T.astype(BF16)
        scores = jnp.dot(pairs, kbd_ref[0, g], preferred_element_type=F32) * (1.0 / math.sqrt(HD))
        halves = []
        for e in range(2):
            part = jnp.where(keep, scores[:, e * length : (e + 1) * length], masked_score)
            weights = jnp.exp(part - jnp.max(part, axis=-1, keepdims=True))
            halves.append((weights / jnp.sum(weights, axis=-1, keepdims=True)).astype(BF16))
            p_ref[0, 0, g * 2 * ROWS : (g + 1) * 2 * ROWS, e * length : (e + 1) * length] = halves[e]
        out = jnp.dot(jnp.concatenate(halves, axis=0), vdup_ref[0, g], preferred_element_type=F32)
        for j in range(2):
            even = out[j * ROWS : (j + 1) * ROWS]
            odd = out[(2 + j) * ROWS : (3 + j) * ROWS]
            attn_ref[0, :, g * 256 + j * 128 : g * 256 + (j + 1) * 128] = jnp.where(low, even, odd).astype(BF16)


def forward_parts(x, q, kbd, vdup, gain):
    micro, length, width = x.shape
    chunks = length // ROWS
    return pl.pallas_call(
        forward_kernel,
        grid=(micro, chunks),
        in_specs=[
            pl.BlockSpec((1, ROWS, width), lambda m, c: (m, c, 0)),
            pl.BlockSpec((1, ROWS, HEADS * HD), lambda m, c: (m, c, 0)),
            pl.BlockSpec((1, KVH, 128, 2 * length), lambda m, c: (m, 0, 0, 0)),
            pl.BlockSpec((1, KVH, length, 128), lambda m, c: (m, 0, 0, 0)),
            pl.BlockSpec((1, width), lambda m, c: (0, 0)),
        ],
        out_specs=[
            pl.BlockSpec((1, ROWS, width), lambda m, c: (m, c, 0)),
            pl.BlockSpec((1, 1, KVH * 2 * ROWS, 2 * length), lambda m, c: (m, c, 0, 0)),
            pl.BlockSpec((1, ROWS, HEADS * HD), lambda m, c: (m, c, 0)),
            pl.BlockSpec((1, 1, KVH, 128, 2 * ROWS), lambda m, c: (m, c, 0, 0, 0)),
        ],
        out_shape=[
            jax.ShapeDtypeStruct((micro, length, width), BF16),
            jax.ShapeDtypeStruct((micro, chunks, KVH * 2 * ROWS, 2 * length), BF16),
            jax.ShapeDtypeStruct((micro, length, HEADS * HD), BF16),
            jax.ShapeDtypeStruct((micro, chunks, KVH, 128, 2 * ROWS), BF16),
        ],
        compiler_params=pltpu.CompilerParams(vmem_limit_bytes=24 << 20),
        name="forward_parts",
    )(x, q, kbd, vdup, gain)


def turn_kernel(
    micro, turn, last,
    place_ref, arrived_ref, before_any, cot_any, x_ref, p_ref, qt_ref, kcat_ref, vbd_ref, gain_ref, cs_ref, ct_ref,
    st_ref, wo_ref, wi_ref, acc_in, act_in, qkv_in, up_in,
    act_out, acc_ref, act_any, qkv_any, up_any,
    up_ref, gq_ref, g_ref, cot_sem, up_sem, qkv_sem, act_sem, before_sem,
):
    chunk, active, first, fresh = [place_ref[4 * turn + i] for i in range(4)]
    rows = pl.ds(pl.multiple_of(chunk * ROWS, ROWS), ROWS)
    qd, kvd = HEADS * HD, KVH * HD
    width = up_ref.shape[1]
    length = ct_ref.shape[1]
    if turn:
        old_rows = pl.ds(pl.multiple_of(place_ref[4 * turn - 4] * ROWS, ROWS), ROWS)
        old_active = place_ref[4 * turn - 3]
        keep_before = pltpu.make_async_copy(before_any, act_any.at[micro, old_rows], before_sem)

        @pl.when(old_active == 1)
        def _():
            keep_before.start()

    @pl.when(first == 1)
    def _():
        copy = pltpu.make_async_copy(cot_any.at[micro, rows], up_ref, cot_sem)
        copy.start()
        copy.wait()

    @pl.when(first == 0)
    def _():
        up_ref[...] = arrived_ref[...]

    keep_up = pltpu.make_async_copy(up_ref, up_any.at[micro, rows], up_sem)

    @pl.when(active == 1)
    def _():
        keep_up.start()

    d_attn = [
        jnp.dot(up_ref[...], wo_ref[:, g * 256 : (g + 1) * 256], preferred_element_type=F32)
        for g in range(KVH)
    ]
    low = low_lanes((ROWS, 128))
    cs4 = jnp.concatenate([cs_ref[rows]] * 4, axis=0)
    for g in range(KVH):
        pairs_f = jnp.concatenate([d_attn[g][:, :128], d_attn[g][:, 128:]], axis=0)
        pairs = pairs_f.astype(BF16)
        probs_b = p_ref[micro, chunk, g * 2 * ROWS : (g + 1) * 2 * ROWS, :]
        probs = probs_b.astype(F32)
        d_probs = jnp.dot(pairs, vbd_ref[micro, g], preferred_element_type=F32)
        inner = probs * d_probs
        scores = []
        for e in range(2):
            part = slice(e * length, (e + 1) * length)
            row_inner = jnp.sum(inner[:, part], axis=-1, keepdims=True)
            scores.append((probs[:, part] * (d_probs[:, part] - row_inner) * (1.0 / math.sqrt(HD))).astype(BF16))
        stacked = jnp.concatenate(scores, axis=0)
        turned = jnp.dot(stacked, kcat_ref[micro, g], preferred_element_type=F32) * cs4
        turned = turned + pltpu.roll(turned, HD, 1)
        for j in range(2):
            even = turned[j * ROWS : (j + 1) * ROWS]
            odd = turned[(2 + j) * ROWS : (3 + j) * ROWS]
            gq_ref[:, g * 256 + j * 128 : g * 256 + (j + 1) * 128] = jnp.where(low, even, odd).astype(BF16)
        feats = slice(g * HD, (g + 1) * HD)
        vfeats = slice(kvd + g * HD, kvd + (g + 1) * HD)
        wide = jnp.concatenate(scores, axis=1)
        dk2 = jnp.dot(qt_ref[micro, chunk, g], wide, preferred_element_type=F32)
        dk = dk2[:HD, :length] + dk2[HD:, length:]
        front, back = dk[: HD // 2], dk[HD // 2 :]
        dk = jnp.concatenate(
            [front * ct_ref[...] + back * st_ref[...], back * ct_ref[...] - front * st_ref[...]], axis=0
        )
        dv2 = jnp.dot(pairs.astype(F32).T.astype(BF16), probs_b, preferred_element_type=F32)
        dv = dv2[:HD, :length] + dv2[HD:, length:]
        acc_ref[feats] = jnp.where(fresh == 1, dk, acc_in[feats] + dk)
        acc_ref[vfeats] = jnp.where(fresh == 1, dv, acc_in[vfeats] + dv)
    slab = acc_ref[:, pl.ds(pl.multiple_of((chunk // 2) * 128, 128), 128)].T
    done = jnp.where(chunk % 2 == 1, slab[ROWS:], slab[:ROWS])
    gq_ref[:, qd:] = done.astype(BF16)
    keep_qkv = pltpu.make_async_copy(gq_ref, qkv_any.at[micro, rows], qkv_sem)

    @pl.when(active == 1)
    def _():
        keep_qkv.start()

    x = x_ref[micro, rows].astype(F32)
    inv = lax.rsqrt(jnp.mean(x * x, axis=-1, keepdims=True) + norm_eps)
    total = jnp.zeros((ROWS, 256), F32)
    for n in range(width // 256):
        cols = slice(n * 256, (n + 1) * 256)
        d_normed = jnp.dot(gq_ref[...], wi_ref[:, cols], preferred_element_type=F32)
        scaled = d_normed * gain_ref[:, cols].astype(F32)
        g_ref[:, cols] = scaled
        total = total + scaled * (x_ref[micro, rows, cols].astype(F32) * inv)
    mean = jnp.sum(total, axis=-1, keepdims=True) * (1.0 / width)
    for n in range(width // 256):
        cols = slice(n * 256, (n + 1) * 256)
        unit = x_ref[micro, rows, cols].astype(F32) * inv
        act_out[:, cols] = (up_ref[:, cols].astype(F32) + inv * (g_ref[:, cols] - unit * mean)).astype(BF16)
    if last:
        keep_act = pltpu.make_async_copy(act_out, act_any.at[micro, rows], act_sem)

        @pl.when(active == 1)
        def _():
            keep_act.start()
            keep_act.wait()

    @pl.when(active == 1)
    def _():
        keep_up.wait()
        keep_qkv.wait()

    if turn:

        @pl.when(old_active == 1)
        def _():
            keep_before.wait()


def turn_step(micro, turn, last, place, arrived, before, cot, x, p, qt, kcat, vbd, gain, cs, ct, st, wo, wi, acc, act, qkv, up):
    width = x.shape[-1]
    hbm = pl.BlockSpec(memory_space=pltpu.HBM)
    free = pl.BlockSpec(memory_space=pl.ANY)
    vmem = pl.BlockSpec(memory_space=pltpu.VMEM)
    held = lambda b: pltpu.with_memory_space_constraint(b, pltpu.VMEM)
    apart = lambda b: pltpu.with_memory_space_constraint(b, pltpu.HBM)
    out = lambda b: pltpu.HBM(b.shape, b.dtype)
    return pl.pallas_call(
        functools.partial(turn_kernel, micro, turn, last),
        in_specs=[pl.BlockSpec(memory_space=pltpu.SMEM), vmem, free, hbm, *[vmem] * 12, hbm, hbm, hbm],
        out_specs=[vmem, vmem, hbm, hbm, hbm],
        out_shape=[
            jax.ShapeDtypeStruct((ROWS, width), BF16), pltpu.VMEM(acc.shape, acc.dtype), out(act), out(qkv), out(up),
        ],
        input_output_aliases={16: 2, 17: 3, 18: 4},
        scratch_shapes=[
            pltpu.VMEM((ROWS, width), BF16),
            pltpu.VMEM((ROWS, qkv.shape[-1]), BF16),
            pltpu.VMEM((ROWS, width), F32),
            *[pltpu.SemaphoreType.DMA] * 5,
        ],
        compiler_params=pltpu.CompilerParams(vmem_limit_bytes=8 << 20),
        cost_estimate=pl.CostEstimate(flops=2 * ROWS * width * 2560 * 4, bytes_accessed=12 << 20, transcendentals=0),
        name="turn_step",
    )(
        place, arrived, before, apart(cot), *[held(b) for b in (x, p, qt, kcat, vbd, gain, cs, ct, st, wo, wi, acc)],
        *[apart(b) for b in (act, qkv, up)],
    )


DEPTH = 4


def fsdp_place(i):
    return i // (2 * DEPTH), (i // 2) % DEPTH, i % 2


def fsdp_move(block, dy, dz, dc):
    def target(i):
        y, z, c = fsdp_place(i)
        return (((y + dy) % 2) * DEPTH + (z + dz) % DEPTH) * 2 + (c + dc) % 2

    return lax.ppermute(block, "fsdp", [(i, target(i)) for i in range(lax.axis_size("fsdp"))])


def weight_kernel(block_ref, normed_a, normed_b, up_a, up_b, qkv_a, qkv_b, attn_a, attn_b, *outs):
    dims = (((0,), (0,)), ((), ()))
    qkv = qkv_a.shape[1]
    half = outs[0].shape[1]
    step = pl.program_id(0)
    for left_a, left_b, right_a, right_b, base in (
        (normed_a, normed_b, qkv_a, qkv_b, 0),
        (up_a, up_b, attn_a, attn_b, qkv),
    ):
        for start in range(0, right_a.shape[1], 256):
            cols = slice(start, start + 256)
            value = lax.dot_general(left_a[...], right_a[:, cols], dims, preferred_element_type=F32)
            value += lax.dot_general(left_b[...], right_b[:, cols], dims, preferred_element_type=F32)
            side, place = divmod(base + start, half)
            for pair in range(2):

                @pl.when(step // 2 == pair)
                def _():
                    outs[2 * pair + side][:, place : place + 256] = value.astype(BF16)


def weight_parts(blocks, normed, up, qkv, attn):
    tokens = qkv[0].shape[0]
    half = (qkv[0].shape[1] + attn[0].shape[1]) // 2
    picked = pl.BlockSpec((tokens, 128), lambda i, b: (0, b[i]))
    whole = lambda x: pl.BlockSpec(x.shape, lambda i, b: (0, 0))
    early = pl.BlockSpec((128, half), lambda i, b: (jnp.minimum(i, 1), 0))
    late = pl.BlockSpec((128, half), lambda i, b: (jnp.maximum(i - 2, 0), 0))
    apart = lambda b: pltpu.with_memory_space_constraint(b, pltpu.HBM)
    return pl.pallas_call(
        weight_kernel,
        grid_spec=pltpu.PrefetchScalarGridSpec(
            num_scalar_prefetch=1,
            grid=(4,),
            in_specs=[picked] * 4 + [whole(x) for x in (*qkv, *attn)],
            out_specs=[early, early, late, late],
        ),
        out_shape=[jax.ShapeDtypeStruct((256, half), BF16)] * 4,
        compiler_params=pltpu.CompilerParams(vmem_limit_bytes=32 << 20),
        cost_estimate=pl.CostEstimate(flops=8 * tokens * 512 * 2 * half, bytes_accessed=9 << 20, transcendentals=0),
        name="weight_parts",
    )(blocks, *[apart(b) for b in (*normed, *up, *qkv, *attn)])


def added(a, b):
    return (a.astype(F32) + b.astype(F32)).astype(BF16)


def weight_sums(normed, up, qkv, attn):
    y, z, c = fsdp_place(lax.axis_index("fsdp"))

    def parts(*moves):
        bases = [2 * ((z + dz) % DEPTH) + c for dz in moves]
        return weight_parts(
            jnp.stack([base + 2 * DEPTH * i for base in bases for i in range(2)]), normed, up, qkv, attn
        )

    left1, right3, left3, right1 = parts(-1, 1)
    up_sum, down_sum = fsdp_move(left1, 0, 1, 0), fsdp_move(right1, 0, -1, 0)
    left2, right2, left0, right0 = parts(2, 0)
    up_sum, down_sum = added(up_sum, left2), added(down_sum, right2)
    up_sum, down_sum = fsdp_move(up_sum, 0, 1, 0), fsdp_move(down_sum, 0, -1, 0)
    up_sum, down_sum = added(up_sum, left3), added(down_sum, right3)
    up_sum, down_sum = fsdp_move(up_sum, 0, 1, 0), fsdp_move(down_sum, 0, -1, 0)

    def rows(block, which):
        return jnp.where(which == 0, block[:128], block[128:]).astype(F32)

    there = [(rows(s, 1 - y) + rows(t, 1 - y)).astype(BF16) for s, t in ((up_sum, left0), (down_sum, right0))]
    here = [rows(s, y) + rows(t, y) for s, t in ((up_sum, left0), (down_sum, right0))]
    there = fsdp_move(jnp.concatenate(there, axis=1), 1, 0, 0)
    return (jnp.concatenate(here, axis=1) + there.astype(F32)).astype(BF16)


def shard_kernel(wq_ref, wk_ref, wv_ref, wo_ref, out_ref):
    place = 0
    for ref in (wq_ref, wk_ref, wv_ref):
        for start in range(0, ref.shape[1], 128):
            out_ref[place : place + 128] = ref[:, start : start + 128].astype(F32).T.astype(BF16)
            place += 128
    for start in range(0, wo_ref.shape[1], 128):
        out_ref[place : place + 128] = wo_ref[:, start : start + 128]
        place += 128


def shard_blocks(*weights):
    total = sum(b.shape[1] for b in weights)
    return pl.pallas_call(
        shard_kernel,
        out_shape=jax.ShapeDtypeStruct((total, weights[0].shape[0]), BF16),
        compiler_params=pltpu.CompilerParams(vmem_limit_bytes=8 << 20),
        name="shard_blocks",
    )(*[pltpu.with_memory_space_constraint(b, pltpu.HBM) for b in weights])


def arrange_kernel(w_any, wo_ref, wi_ref, *rest):
    sem = rest[-1]
    qkv = wi_ref.shape[0]
    copies = []
    for f in range(w_any.shape[0]):
        own = pl.ds(f * 128, 128)
        copies.append(pltpu.make_async_copy(w_any.at[f, pl.ds(0, qkv)], wi_ref.at[:, own], sem))
        for b in range(wo_ref.shape[1] // 128):
            block = w_any.at[f, pl.ds(qkv + b * 128, 128)]
            copies.append(pltpu.make_async_copy(block, wo_ref.at[own, pl.ds(b * 128, 128)], sem))
    for copy in copies:
        copy.start()
    for copy in copies:
        copy.wait()


def arrange(w, micro, length, width, qd, qkv):
    w = pltpu.with_memory_space_constraint(w, pltpu.HBM)
    hbm = pl.BlockSpec(memory_space=pltpu.HBM)
    vmem = pl.BlockSpec(memory_space=pltpu.VMEM)
    return pl.pallas_call(
        arrange_kernel,
        in_specs=[hbm],
        out_specs=[vmem, vmem, vmem, vmem, hbm, hbm, hbm],
        out_shape=[
            pltpu.VMEM((width, qd), BF16),
            pltpu.VMEM((qkv, width), BF16),
            pltpu.VMEM((2 * KVH * HD, length), F32),
            pltpu.VMEM((ROWS, width), BF16),
            pltpu.HBM((micro, length, width), BF16),
            pltpu.HBM((micro, length, qkv), BF16),
            pltpu.HBM((micro, length, width), BF16),
        ],
        scratch_shapes=[pltpu.SemaphoreType.DMA],
        compiler_params=pltpu.CompilerParams(vmem_limit_bytes=4 << 20),
        name="arrange",
    )(w)


def paired(blocks):
    turned = blocks.transpose(0, 2, 3, 1)
    zero = jnp.zeros_like(turned)
    return jnp.concatenate(
        [jnp.concatenate([turned, zero], axis=3), jnp.concatenate([zero, turned], axis=3)], axis=2
    )


def on_device(x, q, k, v, cot, gain, wq, wk, wv, wo):
    sections = lax.axis_size("section")
    me = lax.axis_index("section")
    x, q, k, v, gain = x[0], q[0], k[0], v[0], gain
    micro, length, width = x.shape
    chunks = length // ROWS
    qd, kvd = HEADS * HD, KVH * HD
    w = lax.all_gather(shard_blocks(wq[0], wk[0], wv[0], wo[0]), "fsdp", axis=0)
    kh = k.reshape(micro, length, KVH, HD)
    vh = v.reshape(micro, length, KVH, HD)
    kg = kh.transpose(0, 2, 1, 3)
    vg = vh.transpose(0, 2, 1, 3)
    swapped = jnp.concatenate([kg[..., HD // 2 :], kg[..., : HD // 2]], axis=-1)
    kcat = jnp.concatenate([kg, swapped], axis=-1)
    vdup = jnp.concatenate([vg, vg], axis=-1)
    cos, sin = rotary_tables(length)
    cs = jnp.concatenate([cos, cos, sin, -sin], axis=1)
    normed, p, attn, qt = forward_parts(x, q, paired(kh), vdup, gain)
    normed, attn = [b.reshape(micro * length, -1) for b in (normed, attn)]
    normed_both, attn_both = (normed, fsdp_move(normed, 0, 0, 1)), (attn, fsdp_move(attn, 0, 0, 1))
    vbd = paired(vh)
    ct, st = cos.T, sin.T
    w, normed_both, attn_both, kcat, vbd, cs, ct, st = lax.optimization_barrier(
        (w, normed_both, attn_both, kcat, vbd, cs, ct, st)
    )
    wo, wi, acc, arrived, act, qkv, up = arrange(w, micro, length, width, qd, qd + 2 * kvd)
    acc, arrived = [acc] * micro, [arrived] * micro
    sent = list(arrived)
    turns = sections - 1 + chunks
    step = jnp.arange(turns, dtype=jnp.int32) - (sections - 1 - me)
    place = jnp.stack(
        [
            chunks - 1 - jnp.clip(step, 0, chunks - 1),
            ((step >= 0) & (step < chunks)).astype(jnp.int32),
            jnp.broadcast_to((me == sections - 1).astype(jnp.int32), (turns,)),
            (step <= 0).astype(jnp.int32),
        ],
        axis=1,
    ).reshape(-1)
    for turn in range(turns):
        for m in range(micro):
            sent[m], acc[m], act, qkv, up = turn_step(
                m, turn, turn == turns - 1, place, arrived[m], sent[m], cot, x, p, qt, kcat, vbd, gain, cs, ct, st, wo, wi,
                acc[m], act, qkv, up,
            )
            if turn < turns - 1:
                arrived[m] = passed_down(sent[m])
    flat = lambda b: b.reshape(micro * length, -1)
    both = lambda b: (b, fsdp_move(b, 0, 0, 1))
    summed = weight_sums(normed_both, both(flat(up)), both(flat(qkv)), attn_both)
    return (
        act[None],
        summed[None, :, :qd],
        summed[None, :, qd : qd + kvd],
        summed[None, :, qd + kvd : qd + 2 * kvd],
        summed[None, :, qd + 2 * kvd :],
    )


def solution(mesh):
    row = P("section", None, "fsdp", None)
    weight = P("section", "fsdp", None)
    return jax.shard_map(
        on_device,
        mesh=mesh,
        in_specs=(row, row, row, row, P(None, "fsdp", None), P("section", None), weight, weight, weight, weight),
        out_specs=(row, weight, weight, weight, weight),
        check_vma=False,
    )
```

```python
import functools
import math

import jax
import jax.numpy as jnp
from jax import lax
from jax.experimental import pallas as pl
from jax.experimental.pallas import tpu as pltpu
from jax.sharding import PartitionSpec as P

HEADS = 16
KVH = 4
HD = 64
ROWS = 64
norm_eps = 1e-05
rotary_base = 500000.0
masked_score = -1e30
F32 = jnp.float32
BF16 = jnp.bfloat16


def passed_down(block):
    size = lax.axis_size("section")
    return lax.ppermute(block, "section", [(i, i - 1) for i in range(1, size)])


def rotary_tables(length):
    half = HD // 2
    inverse = jnp.exp(-(2.0 * jnp.arange(half, dtype=F32) / HD) * math.log(rotary_base))
    angles = jnp.arange(length, dtype=F32)[:, None] * inverse[None, :]
    return jnp.cos(angles), jnp.sin(angles)


def low_lanes(shape):
    return lax.broadcasted_iota(jnp.int32, shape, 1) < HD


def forward_kernel(x_ref, q_ref, kbd_ref, vdup_ref, gain_ref, normed_ref, p_ref, attn_ref, qt_ref):
    chunk = pl.program_id(1)
    x = x_ref[0].astype(F32)
    inv = lax.rsqrt(jnp.mean(x * x, axis=-1, keepdims=True) + norm_eps)
    normed_ref[0] = (x * inv * gain_ref[...].astype(F32)).astype(BF16)
    length = vdup_ref.shape[2]
    shape = (2 * ROWS, length)
    row = lax.broadcasted_iota(jnp.int32, shape, 0)
    row = jnp.where(row >= ROWS, row - ROWS, row) + chunk * ROWS
    keep = row >= lax.broadcasted_iota(jnp.int32, shape, 1)
    low = low_lanes((ROWS, 128))
    for g in range(KVH):
        pairs = jnp.concatenate([q_ref[0, :, g * 256 + j * 128 : g * 256 + (j + 1) * 128] for j in range(2)], axis=0)
        qt_ref[0, 0, g] = pairs.astype(F32).T.astype(BF16)
        scores = jnp.dot(pairs, kbd_ref[0, g], preferred_element_type=F32) * (1.0 / math.sqrt(HD))
        halves = []
        for e in range(2):
            part = jnp.where(keep, scores[:, e * length : (e + 1) * length], masked_score)
            weights = jnp.exp(part - jnp.max(part, axis=-1, keepdims=True))
            halves.append((weights / jnp.sum(weights, axis=-1, keepdims=True)).astype(BF16))
            p_ref[0, 0, g * 2 * ROWS : (g + 1) * 2 * ROWS, e * length : (e + 1) * length] = halves[e]
        out = jnp.dot(jnp.concatenate(halves, axis=0), vdup_ref[0, g], preferred_element_type=F32)
        for j in range(2):
            even = out[j * ROWS : (j + 1) * ROWS]
            odd = out[(2 + j) * ROWS : (3 + j) * ROWS]
            attn_ref[0, :, g * 256 + j * 128 : g * 256 + (j + 1) * 128] = jnp.where(low, even, odd).astype(BF16)


def forward_parts(x, q, kbd, vdup, gain):
    micro, length, width = x.shape
    chunks = length // ROWS
    return pl.pallas_call(
        forward_kernel,
        grid=(micro, chunks),
        in_specs=[
            pl.BlockSpec((1, ROWS, width), lambda m, c: (m, c, 0)),
            pl.BlockSpec((1, ROWS, HEADS * HD), lambda m, c: (m, c, 0)),
            pl.BlockSpec((1, KVH, 128, 2 * length), lambda m, c: (m, 0, 0, 0)),
            pl.BlockSpec((1, KVH, length, 128), lambda m, c: (m, 0, 0, 0)),
            pl.BlockSpec((1, width), lambda m, c: (0, 0)),
        ],
        out_specs=[
            pl.BlockSpec((1, ROWS, width), lambda m, c: (m, c, 0)),
            pl.BlockSpec((1, 1, KVH * 2 * ROWS, 2 * length), lambda m, c: (m, c, 0, 0)),
            pl.BlockSpec((1, ROWS, HEADS * HD), lambda m, c: (m, c, 0)),
            pl.BlockSpec((1, 1, KVH, 128, 2 * ROWS), lambda m, c: (m, c, 0, 0, 0)),
        ],
        out_shape=[
            jax.ShapeDtypeStruct((micro, length, width), BF16),
            jax.ShapeDtypeStruct((micro, chunks, KVH * 2 * ROWS, 2 * length), BF16),
            jax.ShapeDtypeStruct((micro, length, HEADS * HD), BF16),
            jax.ShapeDtypeStruct((micro, chunks, KVH, 128, 2 * ROWS), BF16),
        ],
        compiler_params=pltpu.CompilerParams(vmem_limit_bytes=24 << 20),
        name="forward_parts",
    )(x, q, kbd, vdup, gain)


def turn_kernel(
    micro, turn, last,
    place_ref, arrived_ref, before_any, cot_any, x_ref, p_ref, qt_ref, kcat_ref, vbd_ref, gain_ref, cs_ref, ct_ref,
    st_ref, wo_ref, wi_ref, acc_in, act_in, qkv_in, up_in,
    act_out, acc_ref, act_any, qkv_any, up_any,
    up_ref, gq_ref, g_ref, cot_sem, up_sem, qkv_sem, act_sem, before_sem,
):
    chunk, active, first, fresh = [place_ref[4 * turn + i] for i in range(4)]
    rows = pl.ds(pl.multiple_of(chunk * ROWS, ROWS), ROWS)
    qd, kvd = HEADS * HD, KVH * HD
    width = up_ref.shape[1]
    length = ct_ref.shape[1]
    if turn:
        old_rows = pl.ds(pl.multiple_of(place_ref[4 * turn - 4] * ROWS, ROWS), ROWS)
        old_active = place_ref[4 * turn - 3]
        keep_before = pltpu.make_async_copy(before_any, act_any.at[micro, old_rows], before_sem)

        @pl.when(old_active == 1)
        def _():
            keep_before.start()

    @pl.when(first == 1)
    def _():
        copy = pltpu.make_async_copy(cot_any.at[micro, rows], up_ref, cot_sem)
        copy.start()
        copy.wait()

    @pl.when(first == 0)
    def _():
        up_ref[...] = arrived_ref[...]

    keep_up = pltpu.make_async_copy(up_ref, up_any.at[micro, rows], up_sem)

    @pl.when(active == 1)
    def _():
        keep_up.start()

    d_attn = [
        jnp.dot(up_ref[...], wo_ref[:, g * 256 : (g + 1) * 256], preferred_element_type=F32)
        for g in range(KVH)
    ]
    low = low_lanes((ROWS, 128))
    cs4 = jnp.concatenate([cs_ref[rows]] * 4, axis=0)
    for g in range(KVH):
        pairs_f = jnp.concatenate([d_attn[g][:, :128], d_attn[g][:, 128:]], axis=0)
        pairs = pairs_f.astype(BF16)
        probs_b = p_ref[micro, chunk, g * 2 * ROWS : (g + 1) * 2 * ROWS, :]
        probs = probs_b.astype(F32)
        d_probs = jnp.dot(pairs, vbd_ref[micro, g], preferred_element_type=F32)
        inner = probs * d_probs
        scores = []
        for e in range(2):
            part = slice(e * length, (e + 1) * length)
            row_inner = jnp.sum(inner[:, part], axis=-1, keepdims=True)
            scores.append((probs[:, part] * (d_probs[:, part] - row_inner) * (1.0 / math.sqrt(HD))).astype(BF16))
        stacked = jnp.concatenate(scores, axis=0)
        turned = jnp.dot(stacked, kcat_ref[micro, g], preferred_element_type=F32) * cs4
        turned = turned + pltpu.roll(turned, HD, 1)
        for j in range(2):
            even = turned[j * ROWS : (j + 1) * ROWS]
            odd = turned[(2 + j) * ROWS : (3 + j) * ROWS]
            gq_ref[:, g * 256 + j * 128 : g * 256 + (j + 1) * 128] = jnp.where(low, even, odd).astype(BF16)
        feats = slice(g * HD, (g + 1) * HD)
        vfeats = slice(kvd + g * HD, kvd + (g + 1) * HD)
        wide = jnp.concatenate(scores, axis=1)
        dk2 = jnp.dot(qt_ref[micro, chunk, g], wide, preferred_element_type=F32)
        dk = dk2[:HD, :length] + dk2[HD:, length:]
        front, back = dk[: HD // 2], dk[HD // 2 :]
        dk = jnp.concatenate(
            [front * ct_ref[...] + back * st_ref[...], back * ct_ref[...] - front * st_ref[...]], axis=0
        )
        dv2 = jnp.dot(pairs.astype(F32).T.astype(BF16), probs_b, preferred_element_type=F32)
        dv = dv2[:HD, :length] + dv2[HD:, length:]
        acc_ref[feats] = jnp.where(fresh == 1, dk, acc_in[feats] + dk)
        acc_ref[vfeats] = jnp.where(fresh == 1, dv, acc_in[vfeats] + dv)
    slab = acc_ref[:, pl.ds(pl.multiple_of((chunk // 2) * 128, 128), 128)].T
    done = jnp.where(chunk % 2 == 1, slab[ROWS:], slab[:ROWS])
    gq_ref[:, qd:] = done.astype(BF16)
    keep_qkv = pltpu.make_async_copy(gq_ref, qkv_any.at[micro, rows], qkv_sem)

    @pl.when(active == 1)
    def _():
        keep_qkv.start()

    x = x_ref[micro, rows].astype(F32)
    inv = lax.rsqrt(jnp.mean(x * x, axis=-1, keepdims=True) + norm_eps)
    total = jnp.zeros((ROWS, 256), F32)
    for n in range(width // 256):
        cols = slice(n * 256, (n + 1) * 256)
        d_normed = jnp.dot(gq_ref[...], wi_ref[:, cols], preferred_element_type=F32)
        scaled = d_normed * gain_ref[:, cols].astype(F32)
        g_ref[:, cols] = scaled
        total = total + scaled * (x_ref[micro, rows, cols].astype(F32) * inv)
    mean = jnp.sum(total, axis=-1, keepdims=True) * (1.0 / width)
    for n in range(width // 256):
        cols = slice(n * 256, (n + 1) * 256)
        unit = x_ref[micro, rows, cols].astype(F32) * inv
        act_out[:, cols] = (up_ref[:, cols].astype(F32) + inv * (g_ref[:, cols] - unit * mean)).astype(BF16)
    if last:
        keep_act = pltpu.make_async_copy(act_out, act_any.at[micro, rows], act_sem)

        @pl.when(active == 1)
        def _():
            keep_act.start()
            keep_act.wait()

    @pl.when(active == 1)
    def _():
        keep_up.wait()
        keep_qkv.wait()

    if turn:

        @pl.when(old_active == 1)
        def _():
            keep_before.wait()


def turn_step(micro, turn, last, place, arrived, before, cot, x, p, qt, kcat, vbd, gain, cs, ct, st, wo, wi, acc, act, qkv, up):
    width = x.shape[-1]
    hbm = pl.BlockSpec(memory_space=pltpu.HBM)
    free = pl.BlockSpec(memory_space=pl.ANY)
    vmem = pl.BlockSpec(memory_space=pltpu.VMEM)
    held = lambda b: pltpu.with_memory_space_constraint(b, pltpu.VMEM)
    apart = lambda b: pltpu.with_memory_space_constraint(b, pltpu.HBM)
    out = lambda b: pltpu.HBM(b.shape, b.dtype)
    return pl.pallas_call(
        functools.partial(turn_kernel, micro, turn, last),
        in_specs=[pl.BlockSpec(memory_space=pltpu.SMEM), vmem, free, hbm, *[vmem] * 12, hbm, hbm, hbm],
        out_specs=[vmem, vmem, hbm, hbm, hbm],
        out_shape=[
            jax.ShapeDtypeStruct((ROWS, width), BF16), pltpu.VMEM(acc.shape, acc.dtype), out(act), out(qkv), out(up),
        ],
        input_output_aliases={16: 2, 17: 3, 18: 4},
        scratch_shapes=[
            pltpu.VMEM((ROWS, width), BF16),
            pltpu.VMEM((ROWS, qkv.shape[-1]), BF16),
            pltpu.VMEM((ROWS, width), F32),
            *[pltpu.SemaphoreType.DMA] * 5,
        ],
        compiler_params=pltpu.CompilerParams(vmem_limit_bytes=8 << 20),
        cost_estimate=pl.CostEstimate(flops=2 * ROWS * width * 2560 * 4, bytes_accessed=12 << 20, transcendentals=0),
        name="turn_step",
    )(
        place, arrived, before, apart(cot), *[held(b) for b in (x, p, qt, kcat, vbd, gain, cs, ct, st, wo, wi, acc)],
        *[apart(b) for b in (act, qkv, up)],
    )


DEPTH = 4


def fsdp_place(i):
    return i // (2 * DEPTH), (i // 2) % DEPTH, i % 2


def fsdp_move(block, dy, dz, dc):
    def target(i):
        y, z, c = fsdp_place(i)
        return (((y + dy) % 2) * DEPTH + (z + dz) % DEPTH) * 2 + (c + dc) % 2

    return lax.ppermute(block, "fsdp", [(i, target(i)) for i in range(lax.axis_size("fsdp"))])


def weight_kernel(block_ref, *refs):
    dims = (((0,), (0,)), ((), ()))
    (normed_a, normed_b), (up_a, up_b) = [((x[0], x[1]), (x[2], x[3])) for x in (refs[0:4], refs[4:8])]
    qkv_a, qkv_b, attn_a, attn_b = refs[8:12]
    outs = refs[12:]
    qkv = qkv_a.shape[1]
    half = outs[0].shape[1]
    step = pl.program_id(0)
    for left_a, left_b, right_a, right_b, base in (
        (normed_a, normed_b, qkv_a, qkv_b, 0),
        (up_a, up_b, attn_a, attn_b, qkv),
    ):
        rows_a = jnp.concatenate([x[...] for x in left_a], axis=1)
        rows_b = jnp.concatenate([x[...] for x in left_b], axis=1)
        for start in range(0, right_a.shape[1], 256):
            cols = slice(start, start + 256)
            value = lax.dot_general(rows_a, right_a[:, cols], dims, preferred_element_type=F32)
            value += lax.dot_general(rows_b, right_b[:, cols], dims, preferred_element_type=F32)
            side, place = divmod(base + start, half)
            for pair in range(2):

                @pl.when(step == pair)
                def _():
                    outs[2 * pair + side][:, place : place + 256] = value.astype(BF16)


def weight_parts(blocks, normed, up, qkv, attn):
    tokens = qkv[0].shape[0]
    half = (qkv[0].shape[1] + attn[0].shape[1]) // 2
    picked = [pl.BlockSpec((tokens, 128), lambda i, b, k=k: (0, b[2 * i + k])) for k in range(2)]
    whole = lambda x: pl.BlockSpec(x.shape, lambda i, b: (0, 0))
    out = pl.BlockSpec((256, half), lambda i, b: (0, 0))
    apart = lambda b: pltpu.with_memory_space_constraint(b, pltpu.HBM)
    lefts = [b for pair in (normed, up) for b in pair]
    return pl.pallas_call(
        weight_kernel,
        grid_spec=pltpu.PrefetchScalarGridSpec(
            num_scalar_prefetch=1,
            grid=(2,),
            in_specs=picked * 4 + [whole(x) for x in (*qkv, *attn)],
            out_specs=[out] * 4,
        ),
        out_shape=[jax.ShapeDtypeStruct((256, half), BF16)] * 4,
        compiler_params=pltpu.CompilerParams(vmem_limit_bytes=32 << 20),
        cost_estimate=pl.CostEstimate(flops=8 * tokens * 512 * 2 * half, bytes_accessed=9 << 20, transcendentals=0),
        name="weight_parts",
    )(blocks, *[apart(b) for left in lefts for b in (left, left)], *[apart(b) for b in (*qkv, *attn)])


def added(a, b):
    return (a.astype(F32) + b.astype(F32)).astype(BF16)


def weight_sums(normed, up, qkv, attn):
    y, z, c = fsdp_place(lax.axis_index("fsdp"))

    def parts(*moves):
        bases = [2 * ((z + dz) % DEPTH) + c for dz in moves]
        return weight_parts(
            jnp.stack([base + 2 * DEPTH * i for base in bases for i in range(2)]), normed, up, qkv, attn
        )

    left1, right3, left3, right1 = parts(-1, 1)
    up_sum, down_sum = fsdp_move(left1, 0, 1, 0), fsdp_move(right1, 0, -1, 0)
    left2, right2, left0, right0 = parts(2, 0)
    up_sum, down_sum = added(up_sum, left2), added(down_sum, right2)
    up_sum, down_sum = fsdp_move(up_sum, 0, 1, 0), fsdp_move(down_sum, 0, -1, 0)
    up_sum, down_sum = added(up_sum, left3), added(down_sum, right3)
    up_sum, down_sum = fsdp_move(up_sum, 0, 1, 0), fsdp_move(down_sum, 0, -1, 0)

    def rows(block, which):
        return jnp.where(which == 0, block[:128], block[128:]).astype(F32)

    there = [(rows(s, 1 - y) + rows(t, 1 - y)).astype(BF16) for s, t in ((up_sum, left0), (down_sum, right0))]
    here = [rows(s, y) + rows(t, y) for s, t in ((up_sum, left0), (down_sum, right0))]
    there = fsdp_move(jnp.concatenate(there, axis=1), 1, 0, 0)
    return (jnp.concatenate(here, axis=1) + there.astype(F32)).astype(BF16)


def shard_kernel(wq_ref, wk_ref, wv_ref, wo_ref, out_ref):
    place = 0
    for ref in (wq_ref, wk_ref, wv_ref):
        for start in range(0, ref.shape[1], 128):
            out_ref[place : place + 128] = ref[:, start : start + 128].astype(F32).T.astype(BF16)
            place += 128
    for start in range(0, wo_ref.shape[1], 128):
        out_ref[place : place + 128] = wo_ref[:, start : start + 128]
        place += 128


def shard_blocks(*weights):
    total = sum(b.shape[1] for b in weights)
    return pl.pallas_call(
        shard_kernel,
        out_shape=jax.ShapeDtypeStruct((total, weights[0].shape[0]), BF16),
        compiler_params=pltpu.CompilerParams(vmem_limit_bytes=8 << 20),
        name="shard_blocks",
    )(*[pltpu.with_memory_space_constraint(b, pltpu.HBM) for b in weights])


def gathered(shard, qkv):
    pieces = []

    def around(block, dy):
        below, above = fsdp_move(block, 0, 1, 0), fsdp_move(block, 0, -1, 0)
        pieces.extend([(block, None, (dy, 0, 0)), (below, None, (dy, -1, 0)), (above, None, (dy, 1, 0))])
        far_in, far_out = fsdp_move(below[:qkv], 0, 1, 0), fsdp_move(above[qkv:], 0, -1, 0)
        pieces.extend([(far_in, 0, (dy, 2, 0)), (far_out, 1, (dy, 2, 0))])

    other = fsdp_move(shard, 1, 0, 0)
    around(shard, 0)
    around(other, 1)
    return pieces + [(fsdp_move(b, 0, 0, 1), part, (dy, dz, 1)) for b, part, (dy, dz, _) in pieces]


def arrange_kernel(parts, place_ref, *refs):
    count = len(parts)
    pieces, (wo_ref, wi_ref), sem = refs[:count], refs[count : count + 2], refs[-1]
    qkv = wi_ref.shape[0]
    copies = []
    for k, (piece, part) in enumerate(zip(pieces, parts)):
        own = pl.ds(pl.multiple_of(place_ref[k] * 128, 128), 128)
        if part != 1:
            copies.append(pltpu.make_async_copy(piece.at[pl.ds(0, qkv)], wi_ref.at[:, own], sem))
        if part != 0:
            base = 0 if part == 1 else qkv
            for b in range(wo_ref.shape[1] // 128):
                block = piece.at[pl.ds(base + b * 128, 128)]
                copies.append(pltpu.make_async_copy(block, wo_ref.at[own, pl.ds(b * 128, 128)], sem))
    for copy in copies:
        copy.start()
    for copy in copies:
        copy.wait()


def arrange(pieces, micro, length, width, qd, qkv):
    y, z, c = fsdp_place(lax.axis_index("fsdp"))
    place = jnp.stack(
        [(((y + dy) % 2) * DEPTH + (z + dz) % DEPTH) * 2 + (c + dc) % 2 for _, _, (dy, dz, dc) in pieces]
    )
    hbm = pl.BlockSpec(memory_space=pltpu.HBM)
    free = pl.BlockSpec(memory_space=pl.ANY)
    vmem = pl.BlockSpec(memory_space=pltpu.VMEM)
    return pl.pallas_call(
        functools.partial(arrange_kernel, [part for _, part, _ in pieces]),
        in_specs=[pl.BlockSpec(memory_space=pltpu.SMEM)] + [free] * len(pieces),
        out_specs=[vmem, vmem, vmem, vmem, hbm, hbm, hbm],
        out_shape=[
            pltpu.VMEM((width, qd), BF16),
            pltpu.VMEM((qkv, width), BF16),
            pltpu.VMEM((2 * KVH * HD, length), F32),
            pltpu.VMEM((ROWS, width), BF16),
            pltpu.HBM((micro, length, width), BF16),
            pltpu.HBM((micro, length, qkv), BF16),
            pltpu.HBM((micro, length, width), BF16),
        ],
        scratch_shapes=[pltpu.SemaphoreType.DMA],
        compiler_params=pltpu.CompilerParams(vmem_limit_bytes=4 << 20),
        name="arrange",
    )(place, *[b for b, _, _ in pieces])


def paired(blocks):
    turned = blocks.transpose(0, 2, 3, 1)
    zero = jnp.zeros_like(turned)
    return jnp.concatenate(
        [jnp.concatenate([turned, zero], axis=3), jnp.concatenate([zero, turned], axis=3)], axis=2
    )


def on_device(x, q, k, v, cot, gain, wq, wk, wv, wo):
    sections = lax.axis_size("section")
    me = lax.axis_index("section")
    x, q, k, v, gain = x[0], q[0], k[0], v[0], gain
    micro, length, width = x.shape
    chunks = length // ROWS
    qd, kvd = HEADS * HD, KVH * HD
    w = gathered(shard_blocks(wq[0], wk[0], wv[0], wo[0]), qd + 2 * kvd)
    kh = k.reshape(micro, length, KVH, HD)
    vh = v.reshape(micro, length, KVH, HD)
    kg = kh.transpose(0, 2, 1, 3)
    vg = vh.transpose(0, 2, 1, 3)
    swapped = jnp.concatenate([kg[..., HD // 2 :], kg[..., : HD // 2]], axis=-1)
    kcat = jnp.concatenate([kg, swapped], axis=-1)
    vdup = jnp.concatenate([vg, vg], axis=-1)
    cos, sin = rotary_tables(length)
    cs = jnp.concatenate([cos, cos, sin, -sin], axis=1)
    normed, p, attn, qt = forward_parts(x, q, paired(kh), vdup, gain)
    normed, attn = [b.reshape(micro * length, -1) for b in (normed, attn)]
    normed_both, attn_both = (normed, fsdp_move(normed, 0, 0, 1)), (attn, fsdp_move(attn, 0, 0, 1))
    vbd = paired(vh)
    ct, st = cos.T, sin.T
    blocks, normed_both, attn_both, kcat, vbd, cs, ct, st = lax.optimization_barrier(
        ([b for b, _, _ in w], normed_both, attn_both, kcat, vbd, cs, ct, st)
    )
    w = [(b, part, move) for b, (_, part, move) in zip(blocks, w)]
    wo, wi, acc, arrived, act, qkv, up = arrange(w, micro, length, width, qd, qd + 2 * kvd)
    acc, arrived = [acc] * micro, [arrived] * micro
    sent = list(arrived)
    turns = sections - 1 + chunks
    step = jnp.arange(turns, dtype=jnp.int32) - (sections - 1 - me)
    place = jnp.stack(
        [
            chunks - 1 - jnp.clip(step, 0, chunks - 1),
            ((step >= 0) & (step < chunks)).astype(jnp.int32),
            jnp.broadcast_to((me == sections - 1).astype(jnp.int32), (turns,)),
            (step <= 0).astype(jnp.int32),
        ],
        axis=1,
    ).reshape(-1)
    for turn in range(turns):
        for m in range(micro):
            sent[m], acc[m], act, qkv, up = turn_step(
                m, turn, turn == turns - 1, place, arrived[m], sent[m], cot, x, p, qt, kcat, vbd, gain, cs, ct, st, wo, wi,
                acc[m], act, qkv, up,
            )
            if turn < turns - 1:
                arrived[m] = passed_down(sent[m])
    flat = lambda b: b.reshape(micro * length, -1)
    both = lambda b: (b, fsdp_move(b, 0, 0, 1))
    summed = weight_sums(normed_both, both(flat(up)), both(flat(qkv)), attn_both)
    return (
        act[None],
        summed[None, :, :qd],
        summed[None, :, qd : qd + kvd],
        summed[None, :, qd + kvd : qd + 2 * kvd],
        summed[None, :, qd + 2 * kvd :],
    )


def solution(mesh):
    row = P("section", None, "fsdp", None)
    weight = P("section", "fsdp", None)
    return jax.shard_map(
        on_device,
        mesh=mesh,
        in_specs=(row, row, row, row, P(None, "fsdp", None), P("section", None), weight, weight, weight, weight),
        out_specs=(row, weight, weight, weight, weight),
        check_vma=False,
    )
```

```python
import functools
import math

import jax
import jax.numpy as jnp
from jax import lax
from jax.experimental import pallas as pl
from jax.experimental.pallas import tpu as pltpu
from jax.sharding import PartitionSpec as P

HEADS = 16
KVH = 4
HD = 64
ROWS = 64
norm_eps = 1e-05
rotary_base = 500000.0
masked_score = -1e30
F32 = jnp.float32
BF16 = jnp.bfloat16


def passed_down(block):
    size = lax.axis_size("section")
    return lax.ppermute(block, "section", [(i, i - 1) for i in range(1, size)])


def rotary_tables(length):
    half = HD // 2
    inverse = jnp.exp(-(2.0 * jnp.arange(half, dtype=F32) / HD) * math.log(rotary_base))
    angles = jnp.arange(length, dtype=F32)[:, None] * inverse[None, :]
    return jnp.cos(angles), jnp.sin(angles)


def low_lanes(shape):
    return lax.broadcasted_iota(jnp.int32, shape, 1) < HD


def forward_kernel(x_ref, q_ref, kbd_ref, vdup_ref, gain_ref, normed_ref, p_ref, attn_ref, qt_ref):
    chunk = pl.program_id(1)
    x = x_ref[0].astype(F32)
    inv = lax.rsqrt(jnp.mean(x * x, axis=-1, keepdims=True) + norm_eps)
    normed_ref[0] = (x * inv * gain_ref[...].astype(F32)).astype(BF16)
    length = vdup_ref.shape[2]
    shape = (2 * ROWS, length)
    row = lax.broadcasted_iota(jnp.int32, shape, 0)
    row = jnp.where(row >= ROWS, row - ROWS, row) + chunk * ROWS
    keep = row >= lax.broadcasted_iota(jnp.int32, shape, 1)
    low = low_lanes((ROWS, 128))
    for g in range(KVH):
        pairs = jnp.concatenate([q_ref[0, :, g * 256 + j * 128 : g * 256 + (j + 1) * 128] for j in range(2)], axis=0)
        qt_ref[0, 0, g] = pairs.astype(F32).T.astype(BF16)
        scores = jnp.dot(pairs, kbd_ref[0, g], preferred_element_type=F32) * (1.0 / math.sqrt(HD))
        halves = []
        for e in range(2):
            part = jnp.where(keep, scores[:, e * length : (e + 1) * length], masked_score)
            weights = jnp.exp(part - jnp.max(part, axis=-1, keepdims=True))
            halves.append((weights / jnp.sum(weights, axis=-1, keepdims=True)).astype(BF16))
            p_ref[0, 0, g * 2 * ROWS : (g + 1) * 2 * ROWS, e * length : (e + 1) * length] = halves[e]
        out = jnp.dot(jnp.concatenate(halves, axis=0), vdup_ref[0, g], preferred_element_type=F32)
        for j in range(2):
            even = out[j * ROWS : (j + 1) * ROWS]
            odd = out[(2 + j) * ROWS : (3 + j) * ROWS]
            attn_ref[0, :, g * 256 + j * 128 : g * 256 + (j + 1) * 128] = jnp.where(low, even, odd).astype(BF16)


def forward_parts(x, q, kbd, vdup, gain):
    micro, length, width = x.shape
    chunks = length // ROWS
    return pl.pallas_call(
        forward_kernel,
        grid=(micro, chunks),
        in_specs=[
            pl.BlockSpec((1, ROWS, width), lambda m, c: (m, c, 0)),
            pl.BlockSpec((1, ROWS, HEADS * HD), lambda m, c: (m, c, 0)),
            pl.BlockSpec((1, KVH, 128, 2 * length), lambda m, c: (m, 0, 0, 0)),
            pl.BlockSpec((1, KVH, length, 128), lambda m, c: (m, 0, 0, 0)),
            pl.BlockSpec((1, width), lambda m, c: (0, 0)),
        ],
        out_specs=[
            pl.BlockSpec((1, ROWS, width), lambda m, c: (m, c, 0)),
            pl.BlockSpec((1, 1, KVH * 2 * ROWS, 2 * length), lambda m, c: (m, c, 0, 0)),
            pl.BlockSpec((1, ROWS, HEADS * HD), lambda m, c: (m, c, 0)),
            pl.BlockSpec((1, 1, KVH, 128, 2 * ROWS), lambda m, c: (m, c, 0, 0, 0)),
        ],
        out_shape=[
            jax.ShapeDtypeStruct((micro, length, width), BF16),
            jax.ShapeDtypeStruct((micro, chunks, KVH * 2 * ROWS, 2 * length), BF16),
            jax.ShapeDtypeStruct((micro, length, HEADS * HD), BF16),
            jax.ShapeDtypeStruct((micro, chunks, KVH, 128, 2 * ROWS), BF16),
        ],
        compiler_params=pltpu.CompilerParams(vmem_limit_bytes=24 << 20),
        name="forward_parts",
    )(x, q, kbd, vdup, gain)


def turn_kernel(
    micro, turn, last,
    place_ref, arrived_ref, before_any, cot_any, x_ref, p_ref, qt_ref, kcat_ref, vbd_ref, gain_ref, cs_ref, ct_ref,
    st_ref, wo_ref, wi_ref, acc_in, act_in, qkv_in, up_in,
    act_out, acc_ref, act_any, qkv_any, up_any,
    up_ref, gq_ref, g_ref, cot_sem, up_sem, qkv_sem, act_sem, before_sem,
):
    chunk, active, first, fresh = [place_ref[4 * turn + i] for i in range(4)]
    rows = pl.ds(pl.multiple_of(chunk * ROWS, ROWS), ROWS)
    qd, kvd = HEADS * HD, KVH * HD
    width = up_ref.shape[1]
    length = ct_ref.shape[1]
    if turn:
        old_rows = pl.ds(pl.multiple_of(place_ref[4 * turn - 4] * ROWS, ROWS), ROWS)
        old_active = place_ref[4 * turn - 3]
        keep_before = pltpu.make_async_copy(before_any, act_any.at[micro, old_rows], before_sem)

        @pl.when(old_active == 1)
        def _():
            keep_before.start()

    @pl.when(first == 1)
    def _():
        copy = pltpu.make_async_copy(cot_any.at[micro, rows], up_ref, cot_sem)
        copy.start()
        copy.wait()

    @pl.when(first == 0)
    def _():
        up_ref[...] = arrived_ref[...]

    keep_up = pltpu.make_async_copy(up_ref, up_any.at[rows], up_sem)

    @pl.when(active == 1)
    def _():
        keep_up.start()

    d_attn = [
        jnp.dot(up_ref[...], wo_ref[:, g * 256 : (g + 1) * 256], preferred_element_type=F32)
        for g in range(KVH)
    ]
    low = low_lanes((ROWS, 128))
    cs4 = jnp.concatenate([cs_ref[rows]] * 4, axis=0)
    groups = range(KVH)
    pairs = [jnp.concatenate([d[:, :128], d[:, 128:]], axis=0).astype(BF16) for d in d_attn]
    d_probs = [jnp.dot(pairs[g], vbd_ref[micro, g], preferred_element_type=F32) for g in groups]
    probs = [p_ref[micro, chunk, g * 2 * ROWS : (g + 1) * 2 * ROWS, :] for g in groups]
    dv2 = [
        jnp.dot(pairs[g].astype(F32).T.astype(BF16), probs[g], preferred_element_type=F32) for g in groups
    ]
    scores = []
    for g in groups:
        probs_f = probs[g].astype(F32)
        halves = []
        for e in range(2):
            part = slice(e * length, (e + 1) * length)
            row_inner = jnp.sum(probs_f[:, part] * d_probs[g][:, part], axis=-1, keepdims=True)
            scaled = probs_f[:, part] * (d_probs[g][:, part] - row_inner) * (1.0 / math.sqrt(HD))
            halves.append(scaled.astype(BF16))
        scores.append(halves)
    dk2 = [
        jnp.dot(qt_ref[micro, chunk, g], jnp.concatenate(scores[g], axis=1), preferred_element_type=F32)
        for g in groups
    ]
    turned = [
        jnp.dot(jnp.concatenate(scores[g], axis=0), kcat_ref[micro, g], preferred_element_type=F32) for g in groups
    ]
    cos_rows, sin_rows = ct_ref[...], st_ref[...]
    for g in groups:
        dk = dk2[g][:HD, :length] + dk2[g][HD:, length:]
        front, back = dk[: HD // 2], dk[HD // 2 :]
        dk = jnp.concatenate([front * cos_rows + back * sin_rows, back * cos_rows - front * sin_rows], axis=0)
        dv = dv2[g][:HD, :length] + dv2[g][HD:, length:]
        for feats, value in ((slice(g * HD, (g + 1) * HD), dk), (slice(kvd + g * HD, kvd + (g + 1) * HD), dv)):
            acc_ref[feats] = jnp.where(fresh == 1, value, acc_in[feats] + value)
    for g in groups:
        spun = turned[g] * cs4
        spun = spun + pltpu.roll(spun, HD, 1)
        for j in range(2):
            even = spun[j * ROWS : (j + 1) * ROWS]
            odd = spun[(2 + j) * ROWS : (3 + j) * ROWS]
            gq_ref[:, g * 256 + j * 128 : g * 256 + (j + 1) * 128] = jnp.where(low, even, odd).astype(BF16)
    slab = acc_ref[:, pl.ds(pl.multiple_of((chunk // 2) * 128, 128), 128)].T
    done = jnp.where(chunk % 2 == 1, slab[ROWS:], slab[:ROWS])
    gq_ref[:, qd:] = done.astype(BF16)
    keep_qkv = pltpu.make_async_copy(gq_ref, qkv_any.at[rows], qkv_sem)

    @pl.when(active == 1)
    def _():
        keep_qkv.start()

    x = x_ref[micro, rows].astype(F32)
    inv = lax.rsqrt(jnp.mean(x * x, axis=-1, keepdims=True) + norm_eps)
    total = jnp.zeros((ROWS, 256), F32)
    for n in range(width // 256):
        cols = slice(n * 256, (n + 1) * 256)
        d_normed = jnp.dot(gq_ref[...], wi_ref[:, cols], preferred_element_type=F32)
        scaled = d_normed * gain_ref[:, cols].astype(F32)
        g_ref[:, cols] = scaled
        total = total + scaled * (x_ref[micro, rows, cols].astype(F32) * inv)
    mean = jnp.sum(total, axis=-1, keepdims=True) * (1.0 / width)
    for n in range(width // 256):
        cols = slice(n * 256, (n + 1) * 256)
        unit = x_ref[micro, rows, cols].astype(F32) * inv
        act_out[:, cols] = (up_ref[:, cols].astype(F32) + inv * (g_ref[:, cols] - unit * mean)).astype(BF16)
    if last:
        keep_act = pltpu.make_async_copy(act_out, act_any.at[micro, rows], act_sem)

        @pl.when(active == 1)
        def _():
            keep_act.start()
            keep_act.wait()

    @pl.when(active == 1)
    def _():
        keep_up.wait()
        keep_qkv.wait()

    if turn:

        @pl.when(old_active == 1)
        def _():
            keep_before.wait()


def turn_step(micro, turn, last, place, arrived, before, cot, x, p, qt, kcat, vbd, gain, cs, ct, st, wo, wi, acc, act, qkv, up):
    width = x.shape[-1]
    hbm = pl.BlockSpec(memory_space=pltpu.HBM)
    free = pl.BlockSpec(memory_space=pl.ANY)
    vmem = pl.BlockSpec(memory_space=pltpu.VMEM)
    held = lambda b: pltpu.with_memory_space_constraint(b, pltpu.VMEM)
    apart = lambda b: pltpu.with_memory_space_constraint(b, pltpu.HBM)
    out = lambda b: pltpu.HBM(b.shape, b.dtype)
    return pl.pallas_call(
        functools.partial(turn_kernel, micro, turn, last),
        in_specs=[pl.BlockSpec(memory_space=pltpu.SMEM), vmem, free, hbm, *[vmem] * 12, hbm, hbm, hbm],
        out_specs=[vmem, vmem, hbm, hbm, hbm],
        out_shape=[
            jax.ShapeDtypeStruct((ROWS, width), BF16), pltpu.VMEM(acc.shape, acc.dtype), out(act), out(qkv), out(up),
        ],
        input_output_aliases={16: 2, 17: 3, 18: 4},
        scratch_shapes=[
            pltpu.VMEM((ROWS, width), BF16),
            pltpu.VMEM((ROWS, qkv.shape[-1]), BF16),
            pltpu.VMEM((ROWS, width), F32),
            *[pltpu.SemaphoreType.DMA] * 5,
        ],
        compiler_params=pltpu.CompilerParams(vmem_limit_bytes=8 << 20),
        cost_estimate=pl.CostEstimate(flops=2 * ROWS * width * 2560 * 4, bytes_accessed=12 << 20, transcendentals=0),
        name="turn_step",
    )(
        place, arrived, before, apart(cot), *[held(b) for b in (x, p, qt, kcat, vbd, gain, cs, ct, st, wo, wi, acc)],
        *[apart(b) for b in (act, qkv, up)],
    )


DEPTH = 4


def fsdp_place(i):
    return i // (2 * DEPTH), (i // 2) % DEPTH, i % 2


def fsdp_move(block, dy, dz, dc):
    def target(i):
        y, z, c = fsdp_place(i)
        return (((y + dy) % 2) * DEPTH + (z + dz) % DEPTH) * 2 + (c + dc) % 2

    return lax.ppermute(block, "fsdp", [(i, target(i)) for i in range(lax.axis_size("fsdp"))])


def weight_kernel(
    micro, block_ref, normed_a, normed_b, attn_a, attn_b, *refs
):
    ups, qkvs, refs = refs[: 2 * micro], refs[2 * micro : 4 * micro], refs[4 * micro :]
    left_one, right_one, left_two, right_two, normed_cols, up_cols, qkv_rows, attn_rows, turned, sems = refs
    length, qkv = qkvs[0].shape
    tokens = micro * length
    half = left_one.shape[1]
    loads = []
    for core, (normed, attn) in enumerate(((normed_a, attn_a), (normed_b, attn_b))):
        rows = pl.ds(core * tokens, tokens)
        for k in range(4):
            cols, to = pl.ds(pl.multiple_of(block_ref[k] * 128, 128), 128), pl.ds(k * 128, 128)
            loads.append((0, normed.at[:, cols], normed_cols.at[rows, to]))
            for m in range(micro):
                piece = pl.ds(core * tokens + m * length, length)
                loads.append((2, ups[core * micro + m].at[:, cols], up_cols.at[piece, to]))
        for m in range(micro):
            loads.append((1, qkvs[core * micro + m], qkv_rows.at[pl.ds(core * tokens + m * length, length)]))
        loads.append((3, attn, attn_rows.at[rows]))
    loads = [
        (kind, pltpu.make_async_copy(source, target, sems.at[k]))
        for k, (kind, source, target) in enumerate(sorted(loads, key=lambda load: load[0]))
    ]
    for _, load in loads:
        load.start()

    def arrived(kind):
        for which, load in loads:
            if which == kind:
                load.wait()

    for kind, left, right, base in ((0, normed_cols, qkv_rows, 0), (2, up_cols, attn_rows, qkv)):
        arrived(kind)
        for start in range(0, left.shape[0], 256):
            turned[:, start : start + 256] = left[start : start + 256].astype(F32).T.astype(BF16)
        arrived(kind + 1)
        for start in range(0, right.shape[1], 256):
            value = jnp.dot(turned[...], right[:, start : start + 256], preferred_element_type=F32).astype(BF16)
            side, place = divmod(base + start, half)
            (left_one, right_one)[side][:, place : place + 256] = value[:256]
            (left_two, right_two)[side][:, place : place + 256] = value[256:]


def weight_parts(blocks, normed, up, qkv, attn):
    tokens = normed[0].shape[0]
    wide, narrow = qkv[0][0].shape[1], attn[0].shape[1]
    half = (wide + narrow) // 2
    free = pl.BlockSpec(memory_space=pl.ANY)
    micro = len(up[0])
    apart = lambda b: pltpu.with_memory_space_constraint(b, pltpu.HBM)
    arrays = [apart(b) for b in (*normed, *attn, *up[0])] + [apart(b) for b in up[1]]
    arrays += [apart(b) for b in qkv[0]] + [apart(b) for b in qkv[1]]
    return pl.pallas_call(
        functools.partial(weight_kernel, micro),
        in_specs=[pl.BlockSpec(memory_space=pltpu.SMEM)] + [free] * len(arrays),
        out_shape=[jax.ShapeDtypeStruct((256, half), BF16)] * 4,
        scratch_shapes=[
            pltpu.VMEM((2 * tokens, 512), BF16),
            pltpu.VMEM((2 * tokens, 512), BF16),
            pltpu.VMEM((2 * tokens, wide), BF16),
            pltpu.VMEM((2 * tokens, narrow), BF16),
            pltpu.VMEM((512, 2 * tokens), BF16),
            pltpu.SemaphoreType.DMA((10 + 10 * micro,)),
        ],
        compiler_params=pltpu.CompilerParams(vmem_limit_bytes=32 << 20),
        cost_estimate=pl.CostEstimate(flops=8 * tokens * 512 * 2 * half, bytes_accessed=9 << 20, transcendentals=0),
        name="weight_parts",
    )(blocks, *arrays)


def added(a, b):
    return (a.astype(F32) + b.astype(F32)).astype(BF16)


def weight_sums(normed, up, qkv, attn):
    y, z, c = fsdp_place(lax.axis_index("fsdp"))

    def parts(*moves):
        bases = [2 * ((z + dz) % DEPTH) + c for dz in moves]
        return weight_parts(
            jnp.stack([base + 2 * DEPTH * i for base in bases for i in range(2)]), normed, up, qkv, attn
        )

    left1, right3, left3, right1 = parts(-1, 1)
    up_sum, down_sum = fsdp_move(left1, 0, 1, 0), fsdp_move(right1, 0, -1, 0)
    left2, right2, left0, right0 = parts(2, 0)
    up_sum, down_sum = added(up_sum, left2), added(down_sum, right2)
    up_sum, down_sum = fsdp_move(up_sum, 0, 1, 0), fsdp_move(down_sum, 0, -1, 0)
    up_sum, down_sum = added(up_sum, left3), added(down_sum, right3)
    up_sum, down_sum = fsdp_move(up_sum, 0, 1, 0), fsdp_move(down_sum, 0, -1, 0)

    def rows(block, which):
        return jnp.where(which == 0, block[:128], block[128:]).astype(F32)

    there = [(rows(s, 1 - y) + rows(t, 1 - y)).astype(BF16) for s, t in ((up_sum, left0), (down_sum, right0))]
    here = [rows(s, y) + rows(t, y) for s, t in ((up_sum, left0), (down_sum, right0))]
    there = fsdp_move(jnp.concatenate(there, axis=1), 1, 0, 0)
    return (jnp.concatenate(here, axis=1) + there.astype(F32)).astype(BF16)


def shard_kernel(wq_ref, wk_ref, wv_ref, wo_ref, out_ref):
    place = 0
    for ref in (wq_ref, wk_ref, wv_ref):
        for start in range(0, ref.shape[1], 128):
            out_ref[place : place + 128] = ref[:, start : start + 128].astype(F32).T.astype(BF16)
            place += 128
    for start in range(0, wo_ref.shape[1], 128):
        out_ref[place : place + 128] = wo_ref[:, start : start + 128]
        place += 128


def shard_blocks(*weights):
    total = sum(b.shape[1] for b in weights)
    return pl.pallas_call(
        shard_kernel,
        out_shape=jax.ShapeDtypeStruct((total, weights[0].shape[0]), BF16),
        compiler_params=pltpu.CompilerParams(vmem_limit_bytes=8 << 20),
        name="shard_blocks",
    )(*[pltpu.with_memory_space_constraint(b, pltpu.HBM) for b in weights])


def gathered(shard, qkv, first, second):
    across = lambda b: fsdp_move(b, 0, 0, 1)
    other, below, above = fsdp_move(shard, 1, 0, 0), fsdp_move(shard, 0, 1, 0), fsdp_move(shard, 0, -1, 0)
    other, below, above, first = lax.optimization_barrier((other, below, above, first))
    other_below, other_above = fsdp_move(other, 0, 1, 0), fsdp_move(other, 0, -1, 0)
    far_in, far_out = fsdp_move(below[:qkv], 0, 1, 0), fsdp_move(above[qkv:], 0, -1, 0)
    beside = second(*first)
    other_below, other_above, far_in, far_out, beside = lax.optimization_barrier(
        (other_below, other_above, far_in, far_out, beside)
    )
    last_in = fsdp_move(other_below[:qkv], 0, 1, 0)
    last_out = fsdp_move(other_above[qkv:], 0, -1, 0)
    arrays = [shard, below, above, other, other_below, other_above, far_in, far_out, last_in, last_out]
    moves = [(0, 0), (0, -1), (0, 1), (1, 0), (1, -1), (1, 1), (0, 2), (0, 2), (1, 2), (1, 2)]
    parts = [None] * 6 + [0, 1, 0, 1]
    places = [
        (k + dc * len(arrays), 0, part, (*move, dc)) for dc in range(2) for k, (part, move) in enumerate(zip(parts, moves))
    ]
    return arrays + [across(b) for b in arrays], places, beside


def arrange_kernel(places, place_ref, *refs):
    count = 1 + max(k for k, _, _, _ in places)
    pieces, (wo_ref, wi_ref), sem = refs[:count], refs[count : count + 2], refs[-1]
    qkv = wi_ref.shape[0]
    copies = []
    for i, (k, row, part, _) in enumerate(places):
        own = pl.ds(pl.multiple_of(place_ref[i] * 128, 128), 128)
        if part != 1:
            copies.append(pltpu.make_async_copy(pieces[k].at[pl.ds(row, qkv)], wi_ref.at[:, own], sem))
            row += qkv
        if part != 0:
            for b in range(wo_ref.shape[1] // 128):
                block = pieces[k].at[pl.ds(row + b * 128, 128)]
                copies.append(pltpu.make_async_copy(block, wo_ref.at[own, pl.ds(b * 128, 128)], sem))
    for copy in copies:
        copy.start()
    for copy in copies:
        copy.wait()


def arrange(arrays, places, micro, length, width, qd, qkv):
    y, z, c = fsdp_place(lax.axis_index("fsdp"))
    place = jnp.stack(
        [(((y + dy) % 2) * DEPTH + (z + dz) % DEPTH) * 2 + (c + dc) % 2 for _, _, _, (dy, dz, dc) in places]
    )
    hbm = pl.BlockSpec(memory_space=pltpu.HBM)
    free = pl.BlockSpec(memory_space=pl.ANY)
    vmem = pl.BlockSpec(memory_space=pltpu.VMEM)
    rows = [pltpu.HBM((length, qkv), BF16)] * micro + [pltpu.HBM((length, width), BF16)] * micro
    wo, wi, acc, arrived, act, *rest = pl.pallas_call(
        functools.partial(arrange_kernel, places),
        in_specs=[pl.BlockSpec(memory_space=pltpu.SMEM)] + [free] * len(arrays),
        out_specs=[vmem, vmem, vmem, vmem, hbm] + [hbm] * len(rows),
        out_shape=[
            pltpu.VMEM((width, qd), BF16),
            pltpu.VMEM((qkv, width), BF16),
            pltpu.VMEM((2 * KVH * HD, length), F32),
            pltpu.VMEM((ROWS, width), BF16),
            pltpu.HBM((micro, length, width), BF16),
            *rows,
        ],
        scratch_shapes=[pltpu.SemaphoreType.DMA],
        compiler_params=pltpu.CompilerParams(vmem_limit_bytes=40 << 20),
        name="arrange",
    )(place, *[pltpu.with_memory_space_constraint(b, pltpu.HBM) for b in arrays])
    return wo, wi, acc, arrived, act, rest[:micro], rest[micro:]


def paired(blocks):
    turned = blocks.transpose(0, 2, 3, 1)
    zero = jnp.zeros_like(turned)
    return jnp.concatenate(
        [jnp.concatenate([turned, zero], axis=3), jnp.concatenate([zero, turned], axis=3)], axis=2
    )


def on_device(x, q, k, v, cot, gain, wq, wk, wv, wo):
    sections = lax.axis_size("section")
    me = lax.axis_index("section")
    x, q, k, v, gain = x[0], q[0], k[0], v[0], gain
    micro, length, width = x.shape
    chunks = length // ROWS
    qd, kvd = HEADS * HD, KVH * HD
    shard = shard_blocks(wq[0], wk[0], wv[0], wo[0])
    turns = sections - 1 + chunks
    step = jnp.arange(turns, dtype=jnp.int32) - (sections - 1 - me)
    place = jnp.stack(
        [
            chunks - 1 - jnp.clip(step, 0, chunks - 1),
            ((step >= 0) & (step < chunks)).astype(jnp.int32),
            jnp.broadcast_to((me == sections - 1).astype(jnp.int32), (turns,)),
            (step <= 0).astype(jnp.int32),
        ],
        axis=1,
    ).reshape(-1)
    kh = k.reshape(micro, length, KVH, HD)
    vh = v.reshape(micro, length, KVH, HD)
    kg = kh.transpose(0, 2, 1, 3)
    vg = vh.transpose(0, 2, 1, 3)
    cos, sin = rotary_tables(length)
    swapped_keys = jnp.concatenate([kg[..., HD // 2 :], kg[..., : HD // 2]], axis=-1)
    kcat = jnp.concatenate([kg, swapped_keys], axis=-1)
    tables = (jnp.concatenate([cos, cos, sin, -sin], axis=1), cos.T, sin.T)

    def forward(q, kbd, vdup, vbd, kcat, tables, place):
        normed, p, attn, qt = forward_parts(x, q, kbd, vdup, gain)
        normed, attn = [b.reshape(micro * length, -1) for b in (normed, attn)]
        return normed, p, attn, qt, vbd, kcat, tables, place

    arrays, places, beside = gathered(
        shard,
        qd + 2 * kvd,
        (q, paired(kh), jnp.concatenate([vg, vg], axis=-1), paired(vh), kcat, tables, place),
        forward,
    )
    normed, p, attn, qt, vbd, kcat, (cs, ct, st), place = beside
    normed_both, attn_both = (normed, fsdp_move(normed, 0, 0, 1)), (attn, fsdp_move(attn, 0, 0, 1))
    arrays, normed_both, attn_both = lax.optimization_barrier((arrays, normed_both, attn_both))
    wo, wi, acc, arrived, act, qkv, up = arrange(arrays, places, micro, length, width, qd, qd + 2 * kvd)
    acc, arrived = [acc] * micro, [arrived] * micro
    sent = list(arrived)
    for turn in range(turns):
        for m in range(micro):
            sent[m], acc[m], act, qkv[m], up[m] = turn_step(
                m, turn, turn == turns - 1, place, arrived[m], sent[m], cot, x, p, qt, kcat, vbd, gain, cs, ct, st, wo, wi,
                acc[m], act, qkv[m], up[m],
            )
            if turn < turns - 1:
                arrived[m] = passed_down(sent[m])
    swapped = [[fsdp_move(b, 0, 0, 1) for b in (up[m], qkv[m])] for m in range(micro)]
    ups, qkvs = [[[own[m] for m in range(micro)], [swapped[m][k] for m in range(micro)]] for k, own in enumerate((up, qkv))]
    summed = weight_sums(normed_both, ups, qkvs, attn_both)
    return (
        act[None],
        summed[None, :, :qd],
        summed[None, :, qd : qd + kvd],
        summed[None, :, qd + kvd : qd + 2 * kvd],
        summed[None, :, qd + 2 * kvd :],
    )


def solution(mesh):
    row = P("section", None, "fsdp", None)
    weight = P("section", "fsdp", None)
    return jax.shard_map(
        on_device,
        mesh=mesh,
        in_specs=(row, row, row, row, P(None, "fsdp", None), P("section", None), weight, weight, weight, weight),
        out_specs=(row, weight, weight, weight, weight),
        check_vma=False,
    )
```

```python
import functools
import math

import jax
import jax.numpy as jnp
from jax import lax
from jax.experimental import pallas as pl
from jax.experimental.pallas import tpu as pltpu
from jax.sharding import PartitionSpec as P

HEADS = 16
KVH = 4
HD = 64
ROWS = 64
norm_eps = 1e-05
rotary_base = 500000.0
masked_score = -1e30
F32 = jnp.float32
BF16 = jnp.bfloat16


def passed_down(block):
    size = lax.axis_size("section")
    return lax.ppermute(block, "section", [(i, i - 1) for i in range(1, size)])


def rotary_tables(length):
    half = HD // 2
    inverse = jnp.exp(-(2.0 * jnp.arange(half, dtype=F32) / HD) * math.log(rotary_base))
    angles = jnp.arange(length, dtype=F32)[:, None] * inverse[None, :]
    return jnp.cos(angles), jnp.sin(angles)


def low_lanes(shape):
    return lax.broadcasted_iota(jnp.int32, shape, 1) < HD


def forward_kernel(x_ref, q_ref, kbd_ref, vdup_ref, gain_ref, normed_ref, p_ref, attn_ref, qt_ref):
    chunk = pl.program_id(1)
    x = x_ref[0].astype(F32)
    inv = lax.rsqrt(jnp.mean(x * x, axis=-1, keepdims=True) + norm_eps)
    normed_ref[0] = (x * inv * gain_ref[...].astype(F32)).astype(BF16)
    length = vdup_ref.shape[2]
    shape = (2 * ROWS, length)
    row = lax.broadcasted_iota(jnp.int32, shape, 0)
    row = jnp.where(row >= ROWS, row - ROWS, row) + chunk * ROWS
    keep = row >= lax.broadcasted_iota(jnp.int32, shape, 1)
    low = low_lanes((ROWS, 128))
    for g in range(KVH):
        pairs = jnp.concatenate([q_ref[0, :, g * 256 + j * 128 : g * 256 + (j + 1) * 128] for j in range(2)], axis=0)
        qt_ref[0, 0, g] = pairs.astype(F32).T.astype(BF16)
        scores = jnp.dot(pairs, kbd_ref[0, g], preferred_element_type=F32) * (1.0 / math.sqrt(HD))
        halves = []
        for e in range(2):
            part = jnp.where(keep, scores[:, e * length : (e + 1) * length], masked_score)
            weights = jnp.exp(part - jnp.max(part, axis=-1, keepdims=True))
            halves.append((weights / jnp.sum(weights, axis=-1, keepdims=True)).astype(BF16))
            p_ref[0, 0, g * 2 * ROWS : (g + 1) * 2 * ROWS, e * length : (e + 1) * length] = halves[e]
        out = jnp.dot(jnp.concatenate(halves, axis=0), vdup_ref[0, g], preferred_element_type=F32)
        for j in range(2):
            even = out[j * ROWS : (j + 1) * ROWS]
            odd = out[(2 + j) * ROWS : (3 + j) * ROWS]
            attn_ref[0, :, g * 256 + j * 128 : g * 256 + (j + 1) * 128] = jnp.where(low, even, odd).astype(BF16)


def forward_parts(x, q, kbd, vdup, gain):
    micro, length, width = x.shape
    chunks = length // ROWS
    return pl.pallas_call(
        forward_kernel,
        grid=(micro, chunks),
        in_specs=[
            pl.BlockSpec((1, ROWS, width), lambda m, c: (m, c, 0)),
            pl.BlockSpec((1, ROWS, HEADS * HD), lambda m, c: (m, c, 0)),
            pl.BlockSpec((1, KVH, 128, 2 * length), lambda m, c: (m, 0, 0, 0)),
            pl.BlockSpec((1, KVH, length, 128), lambda m, c: (m, 0, 0, 0)),
            pl.BlockSpec((1, width), lambda m, c: (0, 0)),
        ],
        out_specs=[
            pl.BlockSpec((1, ROWS, width), lambda m, c: (m, c, 0)),
            pl.BlockSpec((1, 1, KVH * 2 * ROWS, 2 * length), lambda m, c: (m, c, 0, 0)),
            pl.BlockSpec((1, ROWS, HEADS * HD), lambda m, c: (m, c, 0)),
            pl.BlockSpec((1, 1, KVH, 128, 2 * ROWS), lambda m, c: (m, c, 0, 0, 0)),
        ],
        out_shape=[
            jax.ShapeDtypeStruct((micro, length, width), BF16),
            jax.ShapeDtypeStruct((micro, chunks, KVH * 2 * ROWS, 2 * length), BF16),
            jax.ShapeDtypeStruct((micro, length, HEADS * HD), BF16),
            jax.ShapeDtypeStruct((micro, chunks, KVH, 128, 2 * ROWS), BF16),
        ],
        compiler_params=pltpu.CompilerParams(vmem_limit_bytes=24 << 20),
        name="forward_parts",
    )(x, q, kbd, vdup, gain)


def turn_kernel(
    micro, turn, last,
    place_ref, arrived_ref, before_any, cot_any, x_ref, p_ref, qt_ref, kcat_ref, vbd_ref, gain_ref, cs_ref, ct_ref,
    st_ref, wo_ref, wi_ref, acc_in, act_in, qkv_in, up_in,
    act_out, acc_ref, act_any, qkv_any, up_any,
    up_ref, gq_ref, g_ref, cot_sem, up_sem, qkv_sem, act_sem, before_sem,
):
    chunk, active, first, fresh = [place_ref[4 * turn + i] for i in range(4)]
    rows = pl.ds(pl.multiple_of(chunk * ROWS, ROWS), ROWS)
    qd, kvd = HEADS * HD, KVH * HD
    width = up_ref.shape[1]
    length = ct_ref.shape[1]
    if turn:
        old_rows = pl.ds(pl.multiple_of(place_ref[4 * turn - 4] * ROWS, ROWS), ROWS)
        old_active = place_ref[4 * turn - 3]
        keep_before = pltpu.make_async_copy(before_any, act_any.at[micro, old_rows], before_sem)

        @pl.when(old_active == 1)
        def _():
            keep_before.start()

    @pl.when(first == 1)
    def _():
        copy = pltpu.make_async_copy(cot_any.at[micro, rows], up_ref, cot_sem)
        copy.start()
        copy.wait()

    @pl.when(first == 0)
    def _():
        up_ref[...] = arrived_ref[...]

    keep_up = pltpu.make_async_copy(up_ref, up_any.at[rows], up_sem)

    @pl.when(active == 1)
    def _():
        keep_up.start()

    d_attn = [
        jnp.dot(up_ref[...], wo_ref[:, g * 256 : (g + 1) * 256], preferred_element_type=F32)
        for g in range(KVH)
    ]
    low = low_lanes((ROWS, 128))
    cs4 = jnp.concatenate([cs_ref[rows]] * 4, axis=0)
    groups = range(KVH)
    pairs = [jnp.concatenate([d[:, :128], d[:, 128:]], axis=0).astype(BF16) for d in d_attn]
    d_probs = [jnp.dot(pairs[g], vbd_ref[micro, g], preferred_element_type=F32) for g in groups]
    probs = [p_ref[micro, chunk, g * 2 * ROWS : (g + 1) * 2 * ROWS, :] for g in groups]
    dv2 = [
        jnp.dot(pairs[g].astype(F32).T.astype(BF16), probs[g], preferred_element_type=F32) for g in groups
    ]
    scores = []
    for g in groups:
        probs_f = probs[g].astype(F32)
        halves = []
        for e in range(2):
            part = slice(e * length, (e + 1) * length)
            row_inner = jnp.sum(probs_f[:, part] * d_probs[g][:, part], axis=-1, keepdims=True)
            scaled = probs_f[:, part] * (d_probs[g][:, part] - row_inner) * (1.0 / math.sqrt(HD))
            halves.append(scaled.astype(BF16))
        scores.append(halves)
    dk2 = [
        jnp.dot(qt_ref[micro, chunk, g], jnp.concatenate(scores[g], axis=1), preferred_element_type=F32)
        for g in groups
    ]
    turned = [
        jnp.dot(jnp.concatenate(scores[g], axis=0), kcat_ref[micro, g], preferred_element_type=F32) for g in groups
    ]
    cos_rows, sin_rows = ct_ref[...], st_ref[...]
    for g in groups:
        dk = dk2[g][:HD, :length] + dk2[g][HD:, length:]
        front, back = dk[: HD // 2], dk[HD // 2 :]
        dk = jnp.concatenate([front * cos_rows + back * sin_rows, back * cos_rows - front * sin_rows], axis=0)
        dv = dv2[g][:HD, :length] + dv2[g][HD:, length:]
        for feats, value in ((slice(g * HD, (g + 1) * HD), dk), (slice(kvd + g * HD, kvd + (g + 1) * HD), dv)):
            acc_ref[feats] = jnp.where(fresh == 1, value, acc_in[feats] + value)
    for g in groups:
        spun = turned[g] * cs4
        spun = spun + pltpu.roll(spun, HD, 1)
        for j in range(2):
            even = spun[j * ROWS : (j + 1) * ROWS]
            odd = spun[(2 + j) * ROWS : (3 + j) * ROWS]
            gq_ref[:, g * 256 + j * 128 : g * 256 + (j + 1) * 128] = jnp.where(low, even, odd).astype(BF16)
    slab = acc_ref[:, pl.ds(pl.multiple_of((chunk // 2) * 128, 128), 128)].T
    done = jnp.where(chunk % 2 == 1, slab[ROWS:], slab[:ROWS])
    gq_ref[:, qd:] = done.astype(BF16)
    keep_qkv = pltpu.make_async_copy(gq_ref, qkv_any.at[rows], qkv_sem)

    @pl.when(active == 1)
    def _():
        keep_qkv.start()

    x = x_ref[micro, rows].astype(F32)
    inv = lax.rsqrt(jnp.mean(x * x, axis=-1, keepdims=True) + norm_eps)
    total = jnp.zeros((ROWS, 256), F32)
    for n in range(width // 256):
        cols = slice(n * 256, (n + 1) * 256)
        d_normed = jnp.dot(gq_ref[...], wi_ref[:, cols], preferred_element_type=F32)
        scaled = d_normed * gain_ref[:, cols].astype(F32)
        g_ref[:, cols] = scaled
        total = total + scaled * (x_ref[micro, rows, cols].astype(F32) * inv)
    mean = jnp.sum(total, axis=-1, keepdims=True) * (1.0 / width)
    for n in range(width // 256):
        cols = slice(n * 256, (n + 1) * 256)
        unit = x_ref[micro, rows, cols].astype(F32) * inv
        act_out[:, cols] = (up_ref[:, cols].astype(F32) + inv * (g_ref[:, cols] - unit * mean)).astype(BF16)
    if last:
        keep_act = pltpu.make_async_copy(act_out, act_any.at[micro, rows], act_sem)

        @pl.when(active == 1)
        def _():
            keep_act.start()
            keep_act.wait()

    @pl.when(active == 1)
    def _():
        keep_up.wait()
        keep_qkv.wait()

    if turn:

        @pl.when(old_active == 1)
        def _():
            keep_before.wait()


def turn_step(micro, turn, last, place, arrived, before, cot, x, p, qt, kcat, vbd, gain, cs, ct, st, wo, wi, acc, act, qkv, up):
    width = x.shape[-1]
    hbm = pl.BlockSpec(memory_space=pltpu.HBM)
    free = pl.BlockSpec(memory_space=pl.ANY)
    vmem = pl.BlockSpec(memory_space=pltpu.VMEM)
    held = lambda b: pltpu.with_memory_space_constraint(b, pltpu.VMEM)
    apart = lambda b: pltpu.with_memory_space_constraint(b, pltpu.HBM)
    out = lambda b: pltpu.HBM(b.shape, b.dtype)
    return pl.pallas_call(
        functools.partial(turn_kernel, micro, turn, last),
        in_specs=[pl.BlockSpec(memory_space=pltpu.SMEM), vmem, free, hbm, *[vmem] * 12, hbm, hbm, hbm],
        out_specs=[vmem, vmem, hbm, hbm, hbm],
        out_shape=[
            jax.ShapeDtypeStruct((ROWS, width), BF16), pltpu.VMEM(acc.shape, acc.dtype), out(act), out(qkv), out(up),
        ],
        input_output_aliases={16: 2, 17: 3, 18: 4},
        scratch_shapes=[
            pltpu.VMEM((ROWS, width), BF16),
            pltpu.VMEM((ROWS, qkv.shape[-1]), BF16),
            pltpu.VMEM((ROWS, width), F32),
            *[pltpu.SemaphoreType.DMA] * 5,
        ],
        compiler_params=pltpu.CompilerParams(vmem_limit_bytes=8 << 20),
        cost_estimate=pl.CostEstimate(flops=2 * ROWS * width * 2560 * 4, bytes_accessed=12 << 20, transcendentals=0),
        name="turn_step",
    )(
        place, arrived, before, apart(cot), *[held(b) for b in (x, p, qt, kcat, vbd, gain, cs, ct, st, wo, wi, acc)],
        *[apart(b) for b in (act, qkv, up)],
    )


DEPTH = 4
PARTS = 4


def fsdp_place(i):
    return i // (2 * DEPTH), (i // 2) % DEPTH, i % 2


def fsdp_move(block, dy, dz, dc):
    def target(i):
        y, z, c = fsdp_place(i)
        return (((y + dy) % 2) * DEPTH + (z + dz) % DEPTH) * 2 + (c + dc) % 2

    return lax.ppermute(block, "fsdp", [(i, target(i)) for i in range(lax.axis_size("fsdp"))])


def weight_kernel(
    micro, block_ref, normed_a, normed_b, attn_a, attn_b, *refs
):
    ups, qkvs, refs = refs[: 2 * micro], refs[2 * micro : 4 * micro], refs[4 * micro :]
    firsts, seconds, refs = refs[:PARTS], refs[PARTS : 2 * PARTS], refs[2 * PARTS :]
    normed_cols, up_cols, qkv_rows, attn_rows, turned, sems = refs
    length, qkv = qkvs[0].shape
    tokens = micro * length
    part = firsts[0].shape[1]
    loads = []
    for core, (normed, attn) in enumerate(((normed_a, attn_a), (normed_b, attn_b))):
        rows = pl.ds(core * tokens, tokens)
        for k in range(4):
            cols, to = pl.ds(pl.multiple_of(block_ref[k] * 128, 128), 128), pl.ds(k * 128, 128)
            loads.append((0, normed.at[:, cols], normed_cols.at[rows, to]))
            for m in range(micro):
                piece = pl.ds(core * tokens + m * length, length)
                loads.append((2, ups[core * micro + m].at[:, cols], up_cols.at[piece, to]))
        for m in range(micro):
            loads.append((1, qkvs[core * micro + m], qkv_rows.at[pl.ds(core * tokens + m * length, length)]))
        loads.append((3, attn, attn_rows.at[rows]))
    loads = [
        (kind, pltpu.make_async_copy(source, target, sems.at[k]))
        for k, (kind, source, target) in enumerate(sorted(loads, key=lambda load: load[0]))
    ]
    for _, load in loads:
        load.start()

    def arrived(kind):
        for which, load in loads:
            if which == kind:
                load.wait()

    for kind, left, right, base in ((0, normed_cols, qkv_rows, 0), (2, up_cols, attn_rows, qkv)):
        arrived(kind)
        for start in range(0, left.shape[0], 256):
            turned[:, start : start + 256] = left[start : start + 256].astype(F32).T.astype(BF16)
        arrived(kind + 1)
        for start in range(0, right.shape[1], 256):
            value = jnp.dot(turned[...], right[:, start : start + 256], preferred_element_type=F32).astype(BF16)
            for piece in range(0, 256, 128):
                which, place = divmod(base + start + piece, part)
                firsts[which][:, place : place + 128] = value[:256, piece : piece + 128]
                seconds[which][:, place : place + 128] = value[256:, piece : piece + 128]


def weight_parts(blocks, normed, up, qkv, attn):
    tokens = normed[0].shape[0]
    wide, narrow = qkv[0][0].shape[1], attn[0].shape[1]
    half = (wide + narrow) // 2
    part = (wide + narrow) // PARTS
    free = pl.BlockSpec(memory_space=pl.ANY)
    micro = len(up[0])
    apart = lambda b: pltpu.with_memory_space_constraint(b, pltpu.HBM)
    arrays = [apart(b) for b in (*normed, *attn, *up[0])] + [apart(b) for b in up[1]]
    arrays += [apart(b) for b in qkv[0]] + [apart(b) for b in qkv[1]]
    return pl.pallas_call(
        functools.partial(weight_kernel, micro),
        in_specs=[pl.BlockSpec(memory_space=pltpu.SMEM)] + [free] * len(arrays),
        out_shape=[jax.ShapeDtypeStruct((256, part), BF16)] * (2 * PARTS),
        scratch_shapes=[
            pltpu.VMEM((2 * tokens, 512), BF16),
            pltpu.VMEM((2 * tokens, 512), BF16),
            pltpu.VMEM((2 * tokens, wide), BF16),
            pltpu.VMEM((2 * tokens, narrow), BF16),
            pltpu.VMEM((512, 2 * tokens), BF16),
            pltpu.SemaphoreType.DMA((10 + 10 * micro,)),
        ],
        compiler_params=pltpu.CompilerParams(vmem_limit_bytes=32 << 20),
        cost_estimate=pl.CostEstimate(flops=8 * tokens * 512 * 2 * half, bytes_accessed=9 << 20, transcendentals=0),
        name="weight_parts",
    )(blocks, *arrays)


def added(a, b):
    return (a.astype(F32) + b.astype(F32)).astype(BF16)


def weight_sums(normed, up, qkv, attn):
    y, z, c = fsdp_place(lax.axis_index("fsdp"))

    def parts(*moves):
        bases = [2 * ((z + dz) % DEPTH) + c for dz in moves]
        return weight_parts(
            jnp.stack([base + 2 * DEPTH * i for base in bases for i in range(2)]), normed, up, qkv, attn
        )

    before, after = (lambda got: (got[:PARTS], got[PARTS:]))(parts(-1, 1))
    way = [1] * (PARTS // 2) + [-1] * (PARTS // 2)
    one = [before[k] if way[k] == 1 else after[k] for k in range(PARTS)]
    three = [after[k] if way[k] == 1 else before[k] for k in range(PARTS)]
    order = [k + h for k in range(PARTS // 2) for h in (0, PARTS // 2)]
    sums = {k: fsdp_move(one[k], 0, way[k], 0) for k in order}
    two, last = (lambda got: (got[:PARTS], got[PARTS:]))(parts(2, 0))
    for term in (two, three):
        sums = {k: fsdp_move(added(sums[k], term[k]), 0, way[k], 0) for k in order}

    def rows(block, which):
        return jnp.where(which == 0, block[:128], block[128:]).astype(F32)

    result = {}
    for k in range(PARTS // 2):
        pair = (k, k + PARTS // 2)
        there = jnp.concatenate([(rows(sums[h], 1 - y) + rows(last[h], 1 - y)).astype(BF16) for h in pair], axis=1)
        there = fsdp_move(there, 1, 0, 0)
        width = there.shape[1] // 2
        for i, h in enumerate(pair):
            here = rows(sums[h], y) + rows(last[h], y)
            result[h] = (here + there[:, i * width : (i + 1) * width].astype(F32)).astype(BF16)
    return jnp.concatenate([result[k] for k in range(PARTS)], axis=1)


def shard_kernel(wq_ref, wk_ref, wv_ref, wo_ref, out_ref):
    place = 0
    for ref in (wq_ref, wk_ref, wv_ref):
        for start in range(0, ref.shape[1], 128):
            out_ref[place : place + 128] = ref[:, start : start + 128].astype(F32).T.astype(BF16)
            place += 128
    for start in range(0, wo_ref.shape[1], 128):
        out_ref[place : place + 128] = wo_ref[:, start : start + 128]
        place += 128


def shard_blocks(*weights):
    total = sum(b.shape[1] for b in weights)
    return pl.pallas_call(
        shard_kernel,
        out_shape=jax.ShapeDtypeStruct((total, weights[0].shape[0]), BF16),
        compiler_params=pltpu.CompilerParams(vmem_limit_bytes=8 << 20),
        name="shard_blocks",
    )(*[pltpu.with_memory_space_constraint(b, pltpu.HBM) for b in weights])


def gathered(shard, qkv, first, second):
    across = lambda b: fsdp_move(b, 0, 0, 1)
    other, below, above = fsdp_move(shard, 1, 0, 0), fsdp_move(shard, 0, 1, 0), fsdp_move(shard, 0, -1, 0)
    other, below, above, first = lax.optimization_barrier((other, below, above, first))
    other_below, other_above = fsdp_move(other, 0, 1, 0), fsdp_move(other, 0, -1, 0)
    far_in, far_out = fsdp_move(below[:qkv], 0, 1, 0), fsdp_move(above[qkv:], 0, -1, 0)
    beside = second(*first)
    next_in, next_out = other_below[:qkv], other_above[qkv:]
    last_in, last_out = fsdp_move(next_in, 0, 1, 0), fsdp_move(next_out, 0, -1, 0)
    shard, below, above, other, far_in, far_out, _ = lax.optimization_barrier(
        (shard, below, above, other, far_in, far_out, (next_in, next_out))
    )
    arrays = [shard, below, above, other, other_below, other_above, far_in, far_out, last_in, last_out]
    moves = [(0, 0), (0, -1), (0, 1), (1, 0), (1, -1), (1, 1), (0, 2), (0, 2), (1, 2), (1, 2)]
    parts = [None] * 6 + [0, 1, 0, 1]
    places = [
        (k + dc * len(arrays), 0, part, (*move, dc)) for dc in range(2) for k, (part, move) in enumerate(zip(parts, moves))
    ]
    return arrays + [across(b) for b in arrays], places, beside


def arrange_kernel(places, place_ref, *refs):
    count = 1 + max(k for k, _, _, _ in places)
    pieces, (wo_ref, wi_ref), sem = refs[:count], refs[count : count + 2], refs[-1]
    qkv = wi_ref.shape[0]
    copies = []
    for i, (k, row, part, _) in enumerate(places):
        own = pl.ds(pl.multiple_of(place_ref[i] * 128, 128), 128)
        if part != 1:
            copies.append(pltpu.make_async_copy(pieces[k].at[pl.ds(row, qkv)], wi_ref.at[:, own], sem))
            row += qkv
        if part != 0:
            for b in range(wo_ref.shape[1] // 128):
                block = pieces[k].at[pl.ds(row + b * 128, 128)]
                copies.append(pltpu.make_async_copy(block, wo_ref.at[own, pl.ds(b * 128, 128)], sem))
    for copy in copies:
        copy.start()
    for copy in copies:
        copy.wait()


def arrange(arrays, places, micro, length, width, qd, qkv):
    y, z, c = fsdp_place(lax.axis_index("fsdp"))
    place = jnp.stack(
        [(((y + dy) % 2) * DEPTH + (z + dz) % DEPTH) * 2 + (c + dc) % 2 for _, _, _, (dy, dz, dc) in places]
    )
    hbm = pl.BlockSpec(memory_space=pltpu.HBM)
    free = pl.BlockSpec(memory_space=pl.ANY)
    vmem = pl.BlockSpec(memory_space=pltpu.VMEM)
    rows = [pltpu.HBM((length, qkv), BF16)] * micro + [pltpu.HBM((length, width), BF16)] * micro
    wo, wi, acc, arrived, act, *rest = pl.pallas_call(
        functools.partial(arrange_kernel, places),
        in_specs=[pl.BlockSpec(memory_space=pltpu.SMEM)] + [free] * len(arrays),
        out_specs=[vmem, vmem, vmem, vmem, hbm] + [hbm] * len(rows),
        out_shape=[
            pltpu.VMEM((width, qd), BF16),
            pltpu.VMEM((qkv, width), BF16),
            pltpu.VMEM((2 * KVH * HD, length), F32),
            pltpu.VMEM((ROWS, width), BF16),
            pltpu.HBM((micro, length, width), BF16),
            *rows,
        ],
        scratch_shapes=[pltpu.SemaphoreType.DMA],
        compiler_params=pltpu.CompilerParams(vmem_limit_bytes=40 << 20),
        name="arrange",
    )(place, *[pltpu.with_memory_space_constraint(b, pltpu.HBM) for b in arrays])
    return wo, wi, acc, arrived, act, rest[:micro], rest[micro:]


def paired(blocks):
    turned = blocks.transpose(0, 2, 3, 1)
    zero = jnp.zeros_like(turned)
    return jnp.concatenate(
        [jnp.concatenate([turned, zero], axis=3), jnp.concatenate([zero, turned], axis=3)], axis=2
    )


def on_device(x, q, k, v, cot, gain, wq, wk, wv, wo):
    sections = lax.axis_size("section")
    me = lax.axis_index("section")
    x, q, k, v, gain = x[0], q[0], k[0], v[0], gain
    micro, length, width = x.shape
    chunks = length // ROWS
    qd, kvd = HEADS * HD, KVH * HD
    shard = shard_blocks(wq[0], wk[0], wv[0], wo[0])
    turns = sections - 1 + chunks
    step = jnp.arange(turns, dtype=jnp.int32) - (sections - 1 - me)
    place = jnp.stack(
        [
            chunks - 1 - jnp.clip(step, 0, chunks - 1),
            ((step >= 0) & (step < chunks)).astype(jnp.int32),
            jnp.broadcast_to((me == sections - 1).astype(jnp.int32), (turns,)),
            (step <= 0).astype(jnp.int32),
        ],
        axis=1,
    ).reshape(-1)
    kh = k.reshape(micro, length, KVH, HD)
    vh = v.reshape(micro, length, KVH, HD)
    kg = kh.transpose(0, 2, 1, 3)
    vg = vh.transpose(0, 2, 1, 3)
    cos, sin = rotary_tables(length)
    swapped_keys = jnp.concatenate([kg[..., HD // 2 :], kg[..., : HD // 2]], axis=-1)
    kcat = jnp.concatenate([kg, swapped_keys], axis=-1)
    tables = (jnp.concatenate([cos, cos, sin, -sin], axis=1), cos.T, sin.T)

    def forward(q, kbd, vdup, vbd, kcat, tables, place):
        normed, p, attn, qt = forward_parts(x, q, kbd, vdup, gain)
        normed, attn = [b.reshape(micro * length, -1) for b in (normed, attn)]
        return normed, p, attn, qt, vbd, kcat, tables, place

    arrays, places, beside = gathered(
        shard,
        qd + 2 * kvd,
        (q, paired(kh), jnp.concatenate([vg, vg], axis=-1), paired(vh), kcat, tables, place),
        forward,
    )
    normed, p, attn, qt, vbd, kcat, (cs, ct, st), place = beside
    normed_both, attn_both = (normed, fsdp_move(normed, 0, 0, 1)), (attn, fsdp_move(attn, 0, 0, 1))
    arrays, normed_both, attn_both = lax.optimization_barrier((arrays, normed_both, attn_both))
    wo, wi, acc, arrived, act, qkv, up = arrange(arrays, places, micro, length, width, qd, qd + 2 * kvd)
    acc, arrived = [acc] * micro, [arrived] * micro
    sent = list(arrived)
    for turn in range(turns):
        for m in range(micro):
            sent[m], acc[m], act, qkv[m], up[m] = turn_step(
                m, turn, turn == turns - 1, place, arrived[m], sent[m], cot, x, p, qt, kcat, vbd, gain, cs, ct, st, wo, wi,
                acc[m], act, qkv[m], up[m],
            )
            if turn < turns - 1:
                arrived[m] = passed_down(sent[m])
    swapped = [[fsdp_move(b, 0, 0, 1) for b in (up[m], qkv[m])] for m in range(micro)]
    ups, qkvs = [[[own[m] for m in range(micro)], [swapped[m][k] for m in range(micro)]] for k, own in enumerate((up, qkv))]
    summed = weight_sums(normed_both, ups, qkvs, attn_both)
    return (
        act[None],
        summed[None, :, :qd],
        summed[None, :, qd : qd + kvd],
        summed[None, :, qd + kvd : qd + 2 * kvd],
        summed[None, :, qd + 2 * kvd :],
    )


def solution(mesh):
    row = P("section", None, "fsdp", None)
    weight = P("section", "fsdp", None)
    return jax.shard_map(
        on_device,
        mesh=mesh,
        in_specs=(row, row, row, row, P(None, "fsdp", None), P("section", None), weight, weight, weight, weight),
        out_specs=(row, weight, weight, weight, weight),
        check_vma=False,
    )
```

```python
import functools
import math

import jax
import jax.numpy as jnp
from jax import lax
from jax.experimental import pallas as pl
from jax.experimental.pallas import tpu as pltpu
from jax.sharding import PartitionSpec as P

HEADS = 16
KVH = 4
HD = 64
ROWS = 64
norm_eps = 1e-05
rotary_base = 500000.0
masked_score = -1e30
F32 = jnp.float32
BF16 = jnp.bfloat16


def passed_down(block):
    size = lax.axis_size("section")
    return lax.ppermute(block, "section", [(i, i - 1) for i in range(1, size)])


def rotary_tables(length):
    half = HD // 2
    inverse = jnp.exp(-(2.0 * jnp.arange(half, dtype=F32) / HD) * math.log(rotary_base))
    angles = jnp.arange(length, dtype=F32)[:, None] * inverse[None, :]
    return jnp.cos(angles), jnp.sin(angles)


def low_lanes(shape):
    return lax.broadcasted_iota(jnp.int32, shape, 1) < HD


def forward_kernel(x_ref, q_ref, kbd_ref, vdup_ref, gain_ref, normed_ref, p_ref, attn_ref, qt_ref):
    chunk = pl.program_id(1)
    x = x_ref[0].astype(F32)
    inv = lax.rsqrt(jnp.mean(x * x, axis=-1, keepdims=True) + norm_eps)
    normed_ref[0] = (x * inv * gain_ref[...].astype(F32)).astype(BF16)
    length = vdup_ref.shape[2]
    shape = (2 * ROWS, length)
    row = lax.broadcasted_iota(jnp.int32, shape, 0)
    row = jnp.where(row >= ROWS, row - ROWS, row) + chunk * ROWS
    keep = row >= lax.broadcasted_iota(jnp.int32, shape, 1)
    low = low_lanes((ROWS, 128))
    for g in range(KVH):
        pairs = jnp.concatenate([q_ref[0, :, g * 256 + j * 128 : g * 256 + (j + 1) * 128] for j in range(2)], axis=0)
        qt_ref[0, 0, g] = pairs.astype(F32).T.astype(BF16)
        scores = jnp.dot(pairs, kbd_ref[0, g], preferred_element_type=F32) * (1.0 / math.sqrt(HD))
        halves = []
        for e in range(2):
            part = jnp.where(keep, scores[:, e * length : (e + 1) * length], masked_score)
            weights = jnp.exp(part - jnp.max(part, axis=-1, keepdims=True))
            halves.append((weights / jnp.sum(weights, axis=-1, keepdims=True)).astype(BF16))
            p_ref[0, 0, g * 2 * ROWS : (g + 1) * 2 * ROWS, e * length : (e + 1) * length] = halves[e]
        out = jnp.dot(jnp.concatenate(halves, axis=0), vdup_ref[0, g], preferred_element_type=F32)
        for j in range(2):
            even = out[j * ROWS : (j + 1) * ROWS]
            odd = out[(2 + j) * ROWS : (3 + j) * ROWS]
            attn_ref[0, :, g * 256 + j * 128 : g * 256 + (j + 1) * 128] = jnp.where(low, even, odd).astype(BF16)


def forward_parts(x, q, kbd, vdup, gain):
    micro, length, width = x.shape
    chunks = length // ROWS
    return pl.pallas_call(
        forward_kernel,
        grid=(micro, chunks),
        in_specs=[
            pl.BlockSpec((1, ROWS, width), lambda m, c: (m, c, 0)),
            pl.BlockSpec((1, ROWS, HEADS * HD), lambda m, c: (m, c, 0)),
            pl.BlockSpec((1, KVH, 128, 2 * length), lambda m, c: (m, 0, 0, 0)),
            pl.BlockSpec((1, KVH, length, 128), lambda m, c: (m, 0, 0, 0)),
            pl.BlockSpec((1, width), lambda m, c: (0, 0)),
        ],
        out_specs=[
            pl.BlockSpec((1, ROWS, width), lambda m, c: (m, c, 0)),
            pl.BlockSpec((1, 1, KVH * 2 * ROWS, 2 * length), lambda m, c: (m, c, 0, 0)),
            pl.BlockSpec((1, ROWS, HEADS * HD), lambda m, c: (m, c, 0)),
            pl.BlockSpec((1, 1, KVH, 128, 2 * ROWS), lambda m, c: (m, c, 0, 0, 0)),
        ],
        out_shape=[
            jax.ShapeDtypeStruct((micro, length, width), BF16),
            jax.ShapeDtypeStruct((micro, chunks, KVH * 2 * ROWS, 2 * length), BF16),
            jax.ShapeDtypeStruct((micro, length, HEADS * HD), BF16),
            jax.ShapeDtypeStruct((micro, chunks, KVH, 128, 2 * ROWS), BF16),
        ],
        compiler_params=pltpu.CompilerParams(vmem_limit_bytes=24 << 20),
        name="forward_parts",
    )(x, q, kbd, vdup, gain)


def turn_kernel(
    micro, turn, last,
    place_ref, arrived_ref, before_any, cot_any, x_ref, p_ref, qt_ref, kcat_ref, vbd_ref, gain_ref, cs_ref, ct_ref,
    st_ref, wo_ref, wi_ref, acc_in, act_in, qkv_in, up_in,
    act_out, acc_ref, act_any, qkv_any, up_any,
    up_ref, gq_ref, g_ref, cot_sem, up_sem, qkv_sem, act_sem, before_sem,
):
    chunk, active, first, fresh = [place_ref[4 * turn + i] for i in range(4)]
    rows = pl.ds(pl.multiple_of(chunk * ROWS, ROWS), ROWS)
    qd, kvd = HEADS * HD, KVH * HD
    width = up_ref.shape[1]
    length = ct_ref.shape[1]
    if turn:
        old_rows = pl.ds(pl.multiple_of(place_ref[4 * turn - 4] * ROWS, ROWS), ROWS)
        old_active = place_ref[4 * turn - 3]
        keep_before = pltpu.make_async_copy(before_any, act_any.at[micro, old_rows], before_sem)

        @pl.when(old_active == 1)
        def _():
            keep_before.start()

    @pl.when(first == 1)
    def _():
        copy = pltpu.make_async_copy(cot_any.at[micro, rows], up_ref, cot_sem)
        copy.start()
        copy.wait()

    @pl.when(first == 0)
    def _():
        up_ref[...] = arrived_ref[...]

    keep_up = pltpu.make_async_copy(up_ref, up_any.at[rows], up_sem)

    @pl.when(active == 1)
    def _():
        keep_up.start()

    d_attn = [
        jnp.dot(up_ref[...], wo_ref[:, g * 256 : (g + 1) * 256], preferred_element_type=F32)
        for g in range(KVH)
    ]
    low = low_lanes((ROWS, 128))
    cs4 = jnp.concatenate([cs_ref[rows]] * 4, axis=0)
    groups = range(KVH)
    pairs = [jnp.concatenate([d[:, :128], d[:, 128:]], axis=0).astype(BF16) for d in d_attn]
    d_probs = [jnp.dot(pairs[g], vbd_ref[micro, g], preferred_element_type=F32) for g in groups]
    probs = [p_ref[micro, chunk, g * 2 * ROWS : (g + 1) * 2 * ROWS, :] for g in groups]
    dv2 = [
        jnp.dot(pairs[g].astype(F32).T.astype(BF16), probs[g], preferred_element_type=F32) for g in groups
    ]
    scores = []
    for g in groups:
        probs_f = probs[g].astype(F32)
        halves = []
        for e in range(2):
            part = slice(e * length, (e + 1) * length)
            row_inner = jnp.sum(probs_f[:, part] * d_probs[g][:, part], axis=-1, keepdims=True)
            scaled = probs_f[:, part] * (d_probs[g][:, part] - row_inner) * (1.0 / math.sqrt(HD))
            halves.append(scaled.astype(BF16))
        scores.append(halves)
    dk2 = [
        jnp.dot(qt_ref[micro, chunk, g], jnp.concatenate(scores[g], axis=1), preferred_element_type=F32)
        for g in groups
    ]
    turned = [
        jnp.dot(jnp.concatenate(scores[g], axis=0), kcat_ref[micro, g], preferred_element_type=F32) for g in groups
    ]
    cos_rows, sin_rows = ct_ref[...], st_ref[...]
    for g in groups:
        dk = dk2[g][:HD, :length] + dk2[g][HD:, length:]
        front, back = dk[: HD // 2], dk[HD // 2 :]
        dk = jnp.concatenate([front * cos_rows + back * sin_rows, back * cos_rows - front * sin_rows], axis=0)
        dv = dv2[g][:HD, :length] + dv2[g][HD:, length:]
        for feats, value in ((slice(g * HD, (g + 1) * HD), dk), (slice(kvd + g * HD, kvd + (g + 1) * HD), dv)):
            acc_ref[feats] = jnp.where(fresh == 1, value, acc_in[feats] + value)
    for g in groups:
        spun = turned[g] * cs4
        spun = spun + pltpu.roll(spun, HD, 1)
        for j in range(2):
            even = spun[j * ROWS : (j + 1) * ROWS]
            odd = spun[(2 + j) * ROWS : (3 + j) * ROWS]
            gq_ref[:, g * 256 + j * 128 : g * 256 + (j + 1) * 128] = jnp.where(low, even, odd).astype(BF16)
    slab = acc_ref[:, pl.ds(pl.multiple_of((chunk // 2) * 128, 128), 128)].T
    done = jnp.where(chunk % 2 == 1, slab[ROWS:], slab[:ROWS])
    gq_ref[:, qd:] = done.astype(BF16)
    keep_qkv = pltpu.make_async_copy(gq_ref, qkv_any.at[rows], qkv_sem)

    @pl.when(active == 1)
    def _():
        keep_qkv.start()

    x = x_ref[micro, rows].astype(F32)
    inv = lax.rsqrt(jnp.mean(x * x, axis=-1, keepdims=True) + norm_eps)
    total = jnp.zeros((ROWS, 256), F32)
    for n in range(width // 256):
        cols = slice(n * 256, (n + 1) * 256)
        d_normed = jnp.dot(gq_ref[...], wi_ref[:, cols], preferred_element_type=F32)
        scaled = d_normed * gain_ref[:, cols].astype(F32)
        g_ref[:, cols] = scaled
        total = total + scaled * (x_ref[micro, rows, cols].astype(F32) * inv)
    mean = jnp.sum(total, axis=-1, keepdims=True) * (1.0 / width)
    for n in range(width // 256):
        cols = slice(n * 256, (n + 1) * 256)
        unit = x_ref[micro, rows, cols].astype(F32) * inv
        act_out[:, cols] = (up_ref[:, cols].astype(F32) + inv * (g_ref[:, cols] - unit * mean)).astype(BF16)
    if last:
        keep_act = pltpu.make_async_copy(act_out, act_any.at[micro, rows], act_sem)

        @pl.when(active == 1)
        def _():
            keep_act.start()
            keep_act.wait()

    @pl.when(active == 1)
    def _():
        keep_up.wait()
        keep_qkv.wait()

    if turn:

        @pl.when(old_active == 1)
        def _():
            keep_before.wait()


def turn_step(micro, turn, last, place, arrived, before, cot, x, p, qt, kcat, vbd, gain, cs, ct, st, wo, wi, acc, act, qkv, up):
    width = x.shape[-1]
    hbm = pl.BlockSpec(memory_space=pltpu.HBM)
    free = pl.BlockSpec(memory_space=pl.ANY)
    vmem = pl.BlockSpec(memory_space=pltpu.VMEM)
    held = lambda b: pltpu.with_memory_space_constraint(b, pltpu.VMEM)
    apart = lambda b: pltpu.with_memory_space_constraint(b, pltpu.HBM)
    out = lambda b: pltpu.HBM(b.shape, b.dtype)
    return pl.pallas_call(
        functools.partial(turn_kernel, micro, turn, last),
        in_specs=[pl.BlockSpec(memory_space=pltpu.SMEM), vmem, free, hbm, *[vmem] * 12, hbm, hbm, hbm],
        out_specs=[vmem, vmem, hbm, hbm, hbm],
        out_shape=[
            jax.ShapeDtypeStruct((ROWS, width), BF16), pltpu.VMEM(acc.shape, acc.dtype), out(act), out(qkv), out(up),
        ],
        input_output_aliases={16: 2, 17: 3, 18: 4},
        scratch_shapes=[
            pltpu.VMEM((ROWS, width), BF16),
            pltpu.VMEM((ROWS, qkv.shape[-1]), BF16),
            pltpu.VMEM((ROWS, width), F32),
            *[pltpu.SemaphoreType.DMA] * 5,
        ],
        compiler_params=pltpu.CompilerParams(vmem_limit_bytes=8 << 20),
        cost_estimate=pl.CostEstimate(flops=2 * ROWS * width * 2560 * 4, bytes_accessed=12 << 20, transcendentals=0),
        name="turn_step",
    )(
        place, arrived, before, apart(cot), *[held(b) for b in (x, p, qt, kcat, vbd, gain, cs, ct, st, wo, wi, acc)],
        *[apart(b) for b in (act, qkv, up)],
    )


DEPTH = 4
PARTS = 4


def fsdp_place(i):
    return i // (2 * DEPTH), (i // 2) % DEPTH, i % 2


def fsdp_move(block, dy, dz, dc):
    def target(i):
        y, z, c = fsdp_place(i)
        return (((y + dy) % 2) * DEPTH + (z + dz) % DEPTH) * 2 + (c + dc) % 2

    return lax.ppermute(block, "fsdp", [(i, target(i)) for i in range(lax.axis_size("fsdp"))])


def weight_kernel(
    micro, block_ref, normed_a, normed_b, attn_a, attn_b, *refs
):
    ups, qkvs, refs = refs[: 2 * micro], refs[2 * micro : 4 * micro], refs[4 * micro :]
    firsts, seconds, refs = refs[:PARTS], refs[PARTS : 2 * PARTS], refs[2 * PARTS :]
    normed_cols, up_cols, qkv_rows, attn_rows, turned, sems = refs
    length, qkv = qkvs[0].shape
    tokens = micro * length
    part = firsts[0].shape[1]
    loads = []
    for core, (normed, attn) in enumerate(((normed_a, attn_a), (normed_b, attn_b))):
        rows = pl.ds(core * tokens, tokens)
        for k in range(4):
            cols, to = pl.ds(pl.multiple_of(block_ref[k] * 128, 128), 128), pl.ds(k * 128, 128)
            loads.append((0, normed.at[:, cols], normed_cols.at[rows, to]))
            for m in range(micro):
                piece = pl.ds(core * tokens + m * length, length)
                loads.append((2, ups[core * micro + m].at[:, cols], up_cols.at[piece, to]))
        for m in range(micro):
            loads.append((1, qkvs[core * micro + m], qkv_rows.at[pl.ds(core * tokens + m * length, length)]))
        loads.append((3, attn, attn_rows.at[rows]))
    loads = [
        (kind, pltpu.make_async_copy(source, target, sems.at[k]))
        for k, (kind, source, target) in enumerate(sorted(loads, key=lambda load: load[0]))
    ]
    for _, load in loads:
        load.start()

    def arrived(kind):
        for which, load in loads:
            if which == kind:
                load.wait()

    for kind, left, right, base in ((0, normed_cols, qkv_rows, 0), (2, up_cols, attn_rows, qkv)):
        arrived(kind)
        for start in range(0, left.shape[0], 256):
            turned[:, start : start + 256] = left[start : start + 256].astype(F32).T.astype(BF16)
        arrived(kind + 1)
        for start in range(0, right.shape[1], 256):
            value = jnp.dot(turned[...], right[:, start : start + 256], preferred_element_type=F32).astype(BF16)
            for piece in range(0, 256, 128):
                which, place = divmod(base + start + piece, part)
                firsts[which][:, place : place + 128] = value[:256, piece : piece + 128]
                seconds[which][:, place : place + 128] = value[256:, piece : piece + 128]


def weight_parts(blocks, normed, up, qkv, attn):
    tokens = normed[0].shape[0]
    wide, narrow = qkv[0][0].shape[1], attn[0].shape[1]
    half = (wide + narrow) // 2
    part = (wide + narrow) // PARTS
    free = pl.BlockSpec(memory_space=pl.ANY)
    micro = len(up[0])
    apart = lambda b: pltpu.with_memory_space_constraint(b, pltpu.HBM)
    arrays = [apart(b) for b in (*normed, *attn, *up[0])] + [apart(b) for b in up[1]]
    arrays += [apart(b) for b in qkv[0]] + [apart(b) for b in qkv[1]]
    return pl.pallas_call(
        functools.partial(weight_kernel, micro),
        in_specs=[pl.BlockSpec(memory_space=pltpu.SMEM)] + [free] * len(arrays),
        out_shape=[jax.ShapeDtypeStruct((256, part), BF16)] * (2 * PARTS),
        scratch_shapes=[
            pltpu.VMEM((2 * tokens, 512), BF16),
            pltpu.VMEM((2 * tokens, 512), BF16),
            pltpu.VMEM((2 * tokens, wide), BF16),
            pltpu.VMEM((2 * tokens, narrow), BF16),
            pltpu.VMEM((512, 2 * tokens), BF16),
            pltpu.SemaphoreType.DMA((10 + 10 * micro,)),
        ],
        compiler_params=pltpu.CompilerParams(vmem_limit_bytes=32 << 20),
        cost_estimate=pl.CostEstimate(flops=8 * tokens * 512 * 2 * half, bytes_accessed=9 << 20, transcendentals=0),
        name="weight_parts",
    )(blocks, *arrays)


def added(a, b):
    return (a.astype(F32) + b.astype(F32)).astype(BF16)


def weight_sums(normed, up, qkv, attn):
    y, z, c = fsdp_place(lax.axis_index("fsdp"))

    def parts(*moves):
        bases = [2 * ((z + dz) % DEPTH) + c for dz in moves]
        return weight_parts(
            jnp.stack([base + 2 * DEPTH * i for base in bases for i in range(2)]), normed, up, qkv, attn
        )

    before, after = (lambda got: (got[:PARTS], got[PARTS:]))(parts(-1, 1))
    way = [1] * (PARTS // 2) + [-1] * (PARTS // 2)
    one = [before[k] if way[k] == 1 else after[k] for k in range(PARTS)]
    three = [after[k] if way[k] == 1 else before[k] for k in range(PARTS)]
    order = [k + h for k in range(PARTS // 2) for h in (0, PARTS // 2)]
    sums = {k: fsdp_move(one[k], 0, way[k], 0) for k in order}
    two, last = (lambda got: (got[:PARTS], got[PARTS:]))(parts(2, 0))
    for term in (two, three):
        sums = {k: fsdp_move(added(sums[k], term[k]), 0, way[k], 0) for k in order}

    def rows(block, which):
        return jnp.where(which == 0, block[:128], block[128:]).astype(F32)

    result = {}
    for k in range(PARTS // 2):
        pair = (k, k + PARTS // 2)
        there = jnp.concatenate([(rows(sums[h], 1 - y) + rows(last[h], 1 - y)).astype(BF16) for h in pair], axis=1)
        there = fsdp_move(there, 1, 0, 0)
        width = there.shape[1] // 2
        for i, h in enumerate(pair):
            here = rows(sums[h], y) + rows(last[h], y)
            result[h] = (here + there[:, i * width : (i + 1) * width].astype(F32)).astype(BF16)
    return jnp.concatenate([result[k] for k in range(PARTS)], axis=1)


def shard_kernel(wq_ref, wk_ref, wv_ref, wo_ref, out_ref):
    place = 0
    for ref in (wq_ref, wk_ref, wv_ref):
        for start in range(0, ref.shape[1], 128):
            out_ref[place : place + 128] = ref[:, start : start + 128].astype(F32).T.astype(BF16)
            place += 128
    for start in range(0, wo_ref.shape[1], 128):
        out_ref[place : place + 128] = wo_ref[:, start : start + 128]
        place += 128


def shard_blocks(*weights):
    total = sum(b.shape[1] for b in weights)
    return pl.pallas_call(
        shard_kernel,
        out_shape=jax.ShapeDtypeStruct((total, weights[0].shape[0]), BF16),
        compiler_params=pltpu.CompilerParams(vmem_limit_bytes=8 << 20),
        name="shard_blocks",
    )(*[pltpu.with_memory_space_constraint(b, pltpu.HBM) for b in weights])


def gathered(shard, qkv, first, second):
    across = lambda b: fsdp_move(b, 0, 0, 1)
    other, below, above = fsdp_move(shard, 1, 0, 0), fsdp_move(shard, 0, 1, 0), fsdp_move(shard, 0, -1, 0)
    other, below, above, first = lax.optimization_barrier((other, below, above, first))
    other_below, other_above = fsdp_move(other, 0, 1, 0), fsdp_move(other, 0, -1, 0)
    far_in, far_out = fsdp_move(below[:qkv], 0, 1, 0), fsdp_move(above[qkv:], 0, -1, 0)
    beside = second(*first)
    other_below, other_above, far_in, far_out, beside = lax.optimization_barrier(
        (other_below, other_above, far_in, far_out, beside)
    )
    next_in, next_out = other_below[:qkv], other_above[qkv:]
    last_in, last_out = fsdp_move(next_in, 0, 1, 0), fsdp_move(next_out, 0, -1, 0)
    shard, below, above, other, far_in, far_out, _ = lax.optimization_barrier(
        (shard, below, above, other, far_in, far_out, (next_in, next_out))
    )
    arrays = [shard, below, above, other, other_below, other_above, far_in, far_out, last_in, last_out]
    moves = [(0, 0), (0, -1), (0, 1), (1, 0), (1, -1), (1, 1), (0, 2), (0, 2), (1, 2), (1, 2)]
    parts = [None] * 6 + [0, 1, 0, 1]
    places = [
        (k + dc * len(arrays), 0, part, (*move, dc)) for dc in range(2) for k, (part, move) in enumerate(zip(parts, moves))
    ]
    return arrays + [across(b) for b in arrays], places, beside


def arrange_kernel(places, place_ref, *refs):
    count = 1 + max(k for k, _, _, _ in places)
    pieces, (wo_ref, wi_ref), sem = refs[:count], refs[count : count + 2], refs[-1]
    qkv = wi_ref.shape[0]
    copies = []
    for i, (k, row, part, _) in enumerate(places):
        own = pl.ds(pl.multiple_of(place_ref[i] * 128, 128), 128)
        if part != 1:
            copies.append(pltpu.make_async_copy(pieces[k].at[pl.ds(row, qkv)], wi_ref.at[:, own], sem))
            row += qkv
        if part != 0:
            for b in range(wo_ref.shape[1] // 128):
                block = pieces[k].at[pl.ds(row + b * 128, 128)]
                copies.append(pltpu.make_async_copy(block, wo_ref.at[own, pl.ds(b * 128, 128)], sem))
    for copy in copies:
        copy.start()
    for copy in copies:
        copy.wait()


def arrange(arrays, places, micro, length, width, qd, qkv):
    y, z, c = fsdp_place(lax.axis_index("fsdp"))
    place = jnp.stack(
        [(((y + dy) % 2) * DEPTH + (z + dz) % DEPTH) * 2 + (c + dc) % 2 for _, _, _, (dy, dz, dc) in places]
    )
    hbm = pl.BlockSpec(memory_space=pltpu.HBM)
    free = pl.BlockSpec(memory_space=pl.ANY)
    vmem = pl.BlockSpec(memory_space=pltpu.VMEM)
    rows = [pltpu.HBM((length, qkv), BF16)] * micro + [pltpu.HBM((length, width), BF16)] * micro
    wo, wi, acc, arrived, act, *rest = pl.pallas_call(
        functools.partial(arrange_kernel, places),
        in_specs=[pl.BlockSpec(memory_space=pltpu.SMEM)] + [free] * len(arrays),
        out_specs=[vmem, vmem, vmem, vmem, hbm] + [hbm] * len(rows),
        out_shape=[
            pltpu.VMEM((width, qd), BF16),
            pltpu.VMEM((qkv, width), BF16),
            pltpu.VMEM((2 * KVH * HD, length), F32),
            pltpu.VMEM((ROWS, width), BF16),
            pltpu.HBM((micro, length, width), BF16),
            *rows,
        ],
        scratch_shapes=[pltpu.SemaphoreType.DMA],
        compiler_params=pltpu.CompilerParams(vmem_limit_bytes=40 << 20),
        name="arrange",
    )(place, *[pltpu.with_memory_space_constraint(b, pltpu.HBM) for b in arrays])
    return wo, wi, acc, arrived, act, rest[:micro], rest[micro:]


def paired(blocks):
    turned = blocks.transpose(0, 2, 3, 1)
    zero = jnp.zeros_like(turned)
    return jnp.concatenate(
        [jnp.concatenate([turned, zero], axis=3), jnp.concatenate([zero, turned], axis=3)], axis=2
    )


def on_device(x, q, k, v, cot, gain, wq, wk, wv, wo):
    sections = lax.axis_size("section")
    me = lax.axis_index("section")
    x, q, k, v, gain = x[0], q[0], k[0], v[0], gain
    micro, length, width = x.shape
    chunks = length // ROWS
    qd, kvd = HEADS * HD, KVH * HD
    shard = shard_blocks(wq[0], wk[0], wv[0], wo[0])
    turns = sections - 1 + chunks
    step = jnp.arange(turns, dtype=jnp.int32) - (sections - 1 - me)
    place = jnp.stack(
        [
            chunks - 1 - jnp.clip(step, 0, chunks - 1),
            ((step >= 0) & (step < chunks)).astype(jnp.int32),
            jnp.broadcast_to((me == sections - 1).astype(jnp.int32), (turns,)),
            (step <= 0).astype(jnp.int32),
        ],
        axis=1,
    ).reshape(-1)
    kh = k.reshape(micro, length, KVH, HD)
    vh = v.reshape(micro, length, KVH, HD)
    kg = kh.transpose(0, 2, 1, 3)
    vg = vh.transpose(0, 2, 1, 3)
    cos, sin = rotary_tables(length)
    swapped_keys = jnp.concatenate([kg[..., HD // 2 :], kg[..., : HD // 2]], axis=-1)
    kcat = jnp.concatenate([kg, swapped_keys], axis=-1)
    tables = (jnp.concatenate([cos, cos, sin, -sin], axis=1), cos.T, sin.T)

    def forward(q, kbd, vdup, vbd, kcat, tables, place):
        normed, p, attn, qt = forward_parts(x, q, kbd, vdup, gain)
        normed, attn = [b.reshape(micro * length, -1) for b in (normed, attn)]
        return normed, p, attn, qt, vbd, kcat, tables, place

    arrays, places, beside = gathered(
        shard,
        qd + 2 * kvd,
        (q, paired(kh), jnp.concatenate([vg, vg], axis=-1), paired(vh), kcat, tables, place),
        forward,
    )
    normed, p, attn, qt, vbd, kcat, (cs, ct, st), place = beside
    normed_both, attn_both = (normed, fsdp_move(normed, 0, 0, 1)), (attn, fsdp_move(attn, 0, 0, 1))
    arrays, normed_both, attn_both = lax.optimization_barrier((arrays, normed_both, attn_both))
    wo, wi, acc, arrived, act, qkv, up = arrange(arrays, places, micro, length, width, qd, qd + 2 * kvd)
    acc, arrived = [acc] * micro, [arrived] * micro
    sent = list(arrived)
    for turn in range(turns):
        for m in range(micro):
            sent[m], acc[m], act, qkv[m], up[m] = turn_step(
                m, turn, turn == turns - 1, place, arrived[m], sent[m], cot, x, p, qt, kcat, vbd, gain, cs, ct, st, wo, wi,
                acc[m], act, qkv[m], up[m],
            )
            if turn < turns - 1:
                arrived[m] = passed_down(sent[m])
    swapped = [[fsdp_move(b, 0, 0, 1) for b in (up[m], qkv[m])] for m in range(micro)]
    ups, qkvs = [[[own[m] for m in range(micro)], [swapped[m][k] for m in range(micro)]] for k, own in enumerate((up, qkv))]
    summed = weight_sums(normed_both, ups, qkvs, attn_both)
    return (
        act[None],
        summed[None, :, :qd],
        summed[None, :, qd : qd + kvd],
        summed[None, :, qd + kvd : qd + 2 * kvd],
        summed[None, :, qd + 2 * kvd :],
    )


def solution(mesh):
    row = P("section", None, "fsdp", None)
    weight = P("section", "fsdp", None)
    return jax.shard_map(
        on_device,
        mesh=mesh,
        in_specs=(row, row, row, row, P(None, "fsdp", None), P("section", None), weight, weight, weight, weight),
        out_specs=(row, weight, weight, weight, weight),
        check_vma=False,
    )
```

```python
import functools
import math

import jax
import jax.numpy as jnp
from jax import lax
from jax.experimental import pallas as pl
from jax.experimental.pallas import tpu as pltpu
from jax.sharding import PartitionSpec as P

HEADS = 16
KVH = 4
HD = 64
ROWS = 64
norm_eps = 1e-05
rotary_base = 500000.0
masked_score = -1e30
F32 = jnp.float32
BF16 = jnp.bfloat16


def passed_down(block):
    size = lax.axis_size("section")
    return lax.ppermute(block, "section", [(i, i - 1) for i in range(1, size)])


def rotary_tables(length):
    half = HD // 2
    inverse = jnp.exp(-(2.0 * jnp.arange(half, dtype=F32) / HD) * math.log(rotary_base))
    angles = jnp.arange(length, dtype=F32)[:, None] * inverse[None, :]
    return jnp.cos(angles), jnp.sin(angles)


def low_lanes(shape):
    return lax.broadcasted_iota(jnp.int32, shape, 1) < HD


def forward_kernel(x_ref, q_ref, kbd_ref, vdup_ref, gain_ref, normed_ref, p_ref, attn_ref, qt_ref):
    chunk = pl.program_id(1)
    x = x_ref[0].astype(F32)
    inv = lax.rsqrt(jnp.mean(x * x, axis=-1, keepdims=True) + norm_eps)
    normed_ref[0] = (x * inv * gain_ref[...].astype(F32)).astype(BF16)
    length = vdup_ref.shape[2]
    shape = (2 * ROWS, length)
    row = lax.broadcasted_iota(jnp.int32, shape, 0)
    row = jnp.where(row >= ROWS, row - ROWS, row) + chunk * ROWS
    keep = row >= lax.broadcasted_iota(jnp.int32, shape, 1)
    low = low_lanes((ROWS, 128))
    for g in range(KVH):
        pairs = jnp.concatenate([q_ref[0, :, g * 256 + j * 128 : g * 256 + (j + 1) * 128] for j in range(2)], axis=0)
        qt_ref[0, 0, g] = pairs.astype(F32).T.astype(BF16)
        scores = jnp.dot(pairs, kbd_ref[0, g], preferred_element_type=F32) * (1.0 / math.sqrt(HD))
        halves = []
        for e in range(2):
            part = jnp.where(keep, scores[:, e * length : (e + 1) * length], masked_score)
            weights = jnp.exp(part - jnp.max(part, axis=-1, keepdims=True))
            halves.append((weights / jnp.sum(weights, axis=-1, keepdims=True)).astype(BF16))
            p_ref[0, 0, g * 2 * ROWS : (g + 1) * 2 * ROWS, e * length : (e + 1) * length] = halves[e]
        out = jnp.dot(jnp.concatenate(halves, axis=0), vdup_ref[0, g], preferred_element_type=F32)
        for j in range(2):
            even = out[j * ROWS : (j + 1) * ROWS]
            odd = out[(2 + j) * ROWS : (3 + j) * ROWS]
            attn_ref[0, :, g * 256 + j * 128 : g * 256 + (j + 1) * 128] = jnp.where(low, even, odd).astype(BF16)


def forward_parts(x, q, kbd, vdup, gain):
    micro, length, width = x.shape
    chunks = length // ROWS
    return pl.pallas_call(
        forward_kernel,
        grid=(micro, chunks),
        in_specs=[
            pl.BlockSpec((1, ROWS, width), lambda m, c: (m, c, 0)),
            pl.BlockSpec((1, ROWS, HEADS * HD), lambda m, c: (m, c, 0)),
            pl.BlockSpec((1, KVH, 128, 2 * length), lambda m, c: (m, 0, 0, 0)),
            pl.BlockSpec((1, KVH, length, 128), lambda m, c: (m, 0, 0, 0)),
            pl.BlockSpec((1, width), lambda m, c: (0, 0)),
        ],
        out_specs=[
            pl.BlockSpec((1, ROWS, width), lambda m, c: (m, c, 0)),
            pl.BlockSpec((1, 1, KVH * 2 * ROWS, 2 * length), lambda m, c: (m, c, 0, 0)),
            pl.BlockSpec((1, ROWS, HEADS * HD), lambda m, c: (m, c, 0)),
            pl.BlockSpec((1, 1, KVH, 128, 2 * ROWS), lambda m, c: (m, c, 0, 0, 0)),
        ],
        out_shape=[
            jax.ShapeDtypeStruct((micro, length, width), BF16),
            jax.ShapeDtypeStruct((micro, chunks, KVH * 2 * ROWS, 2 * length), BF16),
            jax.ShapeDtypeStruct((micro, length, HEADS * HD), BF16),
            jax.ShapeDtypeStruct((micro, chunks, KVH, 128, 2 * ROWS), BF16),
        ],
        compiler_params=pltpu.CompilerParams(vmem_limit_bytes=24 << 20),
        name="forward_parts",
    )(x, q, kbd, vdup, gain)


def turn_kernel(
    micro, turn, last,
    place_ref, arrived_ref, before_any, cot_any, x_ref, p_ref, qt_ref, kcat_ref, vbd_ref, gain_ref, cs_ref, ct_ref,
    st_ref, wo_ref, wi_ref, acc_in, act_in, qkv_in, up_in,
    act_out, acc_ref, act_any, qkv_any, up_any,
    up_ref, gq_ref, g_ref, cot_sem, up_sem, qkv_sem, act_sem, before_sem,
):
    chunk, active, first, fresh = [place_ref[4 * turn + i] for i in range(4)]
    rows = pl.ds(pl.multiple_of(chunk * ROWS, ROWS), ROWS)
    qd, kvd = HEADS * HD, KVH * HD
    width = up_ref.shape[1]
    length = ct_ref.shape[1]
    if turn:
        old_rows = pl.ds(pl.multiple_of(place_ref[4 * turn - 4] * ROWS, ROWS), ROWS)
        old_active = place_ref[4 * turn - 3]
        keep_before = pltpu.make_async_copy(before_any, act_any.at[micro, old_rows], before_sem)

        @pl.when(old_active == 1)
        def _():
            keep_before.start()

    @pl.when(first == 1)
    def _():
        copy = pltpu.make_async_copy(cot_any.at[micro, rows], up_ref, cot_sem)
        copy.start()
        copy.wait()

    @pl.when(first == 0)
    def _():
        up_ref[...] = arrived_ref[...]

    keep_up = pltpu.make_async_copy(up_ref, up_any.at[rows], up_sem)

    @pl.when(active == 1)
    def _():
        keep_up.start()

    d_attn = [
        jnp.dot(up_ref[...], wo_ref[:, g * 256 : (g + 1) * 256], preferred_element_type=F32)
        for g in range(KVH)
    ]
    low = low_lanes((ROWS, 128))
    cs4 = jnp.concatenate([cs_ref[rows]] * 4, axis=0)
    groups = range(KVH)
    pairs = [jnp.concatenate([d[:, :128], d[:, 128:]], axis=0).astype(BF16) for d in d_attn]
    d_probs = [jnp.dot(pairs[g], vbd_ref[micro, g], preferred_element_type=F32) for g in groups]
    probs = [p_ref[micro, chunk, g * 2 * ROWS : (g + 1) * 2 * ROWS, :] for g in groups]
    dv2 = [
        jnp.dot(pairs[g].astype(F32).T.astype(BF16), probs[g], preferred_element_type=F32) for g in groups
    ]
    scores = []
    for g in groups:
        probs_f = probs[g].astype(F32)
        halves = []
        for e in range(2):
            part = slice(e * length, (e + 1) * length)
            row_inner = jnp.sum(probs_f[:, part] * d_probs[g][:, part], axis=-1, keepdims=True)
            scaled = probs_f[:, part] * (d_probs[g][:, part] - row_inner) * (1.0 / math.sqrt(HD))
            halves.append(scaled.astype(BF16))
        scores.append(halves)
    dk2 = [
        jnp.dot(qt_ref[micro, chunk, g], jnp.concatenate(scores[g], axis=1), preferred_element_type=F32)
        for g in groups
    ]
    turned = [
        jnp.dot(jnp.concatenate(scores[g], axis=0), kcat_ref[micro, g], preferred_element_type=F32) for g in groups
    ]
    cos_rows, sin_rows = ct_ref[...], st_ref[...]
    for g in groups:
        dk = dk2[g][:HD, :length] + dk2[g][HD:, length:]
        front, back = dk[: HD // 2], dk[HD // 2 :]
        dk = jnp.concatenate([front * cos_rows + back * sin_rows, back * cos_rows - front * sin_rows], axis=0)
        dv = dv2[g][:HD, :length] + dv2[g][HD:, length:]
        for feats, value in ((slice(g * HD, (g + 1) * HD), dk), (slice(kvd + g * HD, kvd + (g + 1) * HD), dv)):
            acc_ref[feats] = jnp.where(fresh == 1, value, acc_in[feats] + value)
    for g in groups:
        spun = turned[g] * cs4
        spun = spun + pltpu.roll(spun, HD, 1)
        for j in range(2):
            even = spun[j * ROWS : (j + 1) * ROWS]
            odd = spun[(2 + j) * ROWS : (3 + j) * ROWS]
            gq_ref[:, g * 256 + j * 128 : g * 256 + (j + 1) * 128] = jnp.where(low, even, odd).astype(BF16)
    slab = acc_ref[:, pl.ds(pl.multiple_of((chunk // 2) * 128, 128), 128)].T
    done = jnp.where(chunk % 2 == 1, slab[ROWS:], slab[:ROWS])
    gq_ref[:, qd:] = done.astype(BF16)
    keep_qkv = pltpu.make_async_copy(gq_ref, qkv_any.at[rows], qkv_sem)

    @pl.when(active == 1)
    def _():
        keep_qkv.start()

    x = x_ref[micro, rows].astype(F32)
    inv = lax.rsqrt(jnp.mean(x * x, axis=-1, keepdims=True) + norm_eps)
    total = jnp.zeros((ROWS, 256), F32)
    for n in range(width // 256):
        cols = slice(n * 256, (n + 1) * 256)
        d_normed = jnp.dot(gq_ref[...], wi_ref[:, cols], preferred_element_type=F32)
        scaled = d_normed * gain_ref[:, cols].astype(F32)
        g_ref[:, cols] = scaled
        total = total + scaled * (x_ref[micro, rows, cols].astype(F32) * inv)
    mean = jnp.sum(total, axis=-1, keepdims=True) * (1.0 / width)
    for n in range(width // 256):
        cols = slice(n * 256, (n + 1) * 256)
        unit = x_ref[micro, rows, cols].astype(F32) * inv
        act_out[:, cols] = (up_ref[:, cols].astype(F32) + inv * (g_ref[:, cols] - unit * mean)).astype(BF16)
    if last:
        keep_act = pltpu.make_async_copy(act_out, act_any.at[micro, rows], act_sem)

        @pl.when(active == 1)
        def _():
            keep_act.start()
            keep_act.wait()

    @pl.when(active == 1)
    def _():
        keep_up.wait()
        keep_qkv.wait()

    if turn:

        @pl.when(old_active == 1)
        def _():
            keep_before.wait()


def turn_step(micro, turn, last, place, arrived, before, cot, x, p, qt, kcat, vbd, gain, cs, ct, st, wo, wi, acc, act, qkv, up):
    width = x.shape[-1]
    hbm = pl.BlockSpec(memory_space=pltpu.HBM)
    free = pl.BlockSpec(memory_space=pl.ANY)
    vmem = pl.BlockSpec(memory_space=pltpu.VMEM)
    held = lambda b: pltpu.with_memory_space_constraint(b, pltpu.VMEM)
    apart = lambda b: pltpu.with_memory_space_constraint(b, pltpu.HBM)
    out = lambda b: pltpu.HBM(b.shape, b.dtype)
    return pl.pallas_call(
        functools.partial(turn_kernel, micro, turn, last),
        in_specs=[pl.BlockSpec(memory_space=pltpu.SMEM), vmem, free, hbm, *[vmem] * 12, hbm, hbm, hbm],
        out_specs=[vmem, vmem, hbm, hbm, hbm],
        out_shape=[
            jax.ShapeDtypeStruct((ROWS, width), BF16), pltpu.VMEM(acc.shape, acc.dtype), out(act), out(qkv), out(up),
        ],
        input_output_aliases={16: 2, 17: 3, 18: 4},
        scratch_shapes=[
            pltpu.VMEM((ROWS, width), BF16),
            pltpu.VMEM((ROWS, qkv.shape[-1]), BF16),
            pltpu.VMEM((ROWS, width), F32),
            *[pltpu.SemaphoreType.DMA] * 5,
        ],
        compiler_params=pltpu.CompilerParams(vmem_limit_bytes=8 << 20),
        cost_estimate=pl.CostEstimate(flops=2 * ROWS * width * 2560 * 4, bytes_accessed=12 << 20, transcendentals=0),
        name="turn_step",
    )(
        place, arrived, before, apart(cot), *[held(b) for b in (x, p, qt, kcat, vbd, gain, cs, ct, st, wo, wi, acc)],
        *[apart(b) for b in (act, qkv, up)],
    )


DEPTH = 4
PARTS = 4


def fsdp_place(i):
    return i // (2 * DEPTH), (i // 2) % DEPTH, i % 2


def fsdp_move(block, dy, dz, dc):
    def target(i):
        y, z, c = fsdp_place(i)
        return (((y + dy) % 2) * DEPTH + (z + dz) % DEPTH) * 2 + (c + dc) % 2

    return lax.ppermute(block, "fsdp", [(i, target(i)) for i in range(lax.axis_size("fsdp"))])


def weight_kernel(
    micro, block_ref, normed_a, normed_b, attn_a, attn_b, *refs
):
    ups, qkvs, refs = refs[: 2 * micro], refs[2 * micro : 4 * micro], refs[4 * micro :]
    firsts, seconds, refs = refs[:PARTS], refs[PARTS : 2 * PARTS], refs[2 * PARTS :]
    normed_cols, up_cols, qkv_rows, attn_rows, turned, sems = refs
    length, qkv = qkvs[0].shape
    tokens = micro * length
    part = firsts[0].shape[1]
    loads = []
    for core, (normed, attn) in enumerate(((normed_a, attn_a), (normed_b, attn_b))):
        rows = pl.ds(core * tokens, tokens)
        for k in range(4):
            cols, to = pl.ds(pl.multiple_of(block_ref[k] * 128, 128), 128), pl.ds(k * 128, 128)
            loads.append((0, normed.at[:, cols], normed_cols.at[rows, to]))
            for m in range(micro):
                piece = pl.ds(core * tokens + m * length, length)
                loads.append((2, ups[core * micro + m].at[:, cols], up_cols.at[piece, to]))
        for m in range(micro):
            loads.append((1, qkvs[core * micro + m], qkv_rows.at[pl.ds(core * tokens + m * length, length)]))
        loads.append((3, attn, attn_rows.at[rows]))
    loads = [
        (kind, pltpu.make_async_copy(source, target, sems.at[k]))
        for k, (kind, source, target) in enumerate(sorted(loads, key=lambda load: load[0]))
    ]
    for _, load in loads:
        load.start()

    def arrived(kind):
        for which, load in loads:
            if which == kind:
                load.wait()

    for kind, left, right, base in ((0, normed_cols, qkv_rows, 0), (2, up_cols, attn_rows, qkv)):
        arrived(kind)
        for start in range(0, left.shape[0], 256):
            turned[:, start : start + 256] = left[start : start + 256].astype(F32).T.astype(BF16)
        arrived(kind + 1)
        for start in range(0, right.shape[1], 256):
            value = jnp.dot(turned[...], right[:, start : start + 256], preferred_element_type=F32).astype(BF16)
            for piece in range(0, 256, 128):
                which, place = divmod(base + start + piece, part)
                firsts[which][:, place : place + 128] = value[:256, piece : piece + 128]
                seconds[which][:, place : place + 128] = value[256:, piece : piece + 128]


def weight_parts(blocks, normed, up, qkv, attn):
    tokens = normed[0].shape[0]
    wide, narrow = qkv[0][0].shape[1], attn[0].shape[1]
    half = (wide + narrow) // 2
    part = (wide + narrow) // PARTS
    free = pl.BlockSpec(memory_space=pl.ANY)
    micro = len(up[0])
    apart = lambda b: pltpu.with_memory_space_constraint(b, pltpu.HBM)
    arrays = [apart(b) for b in (*normed, *attn, *up[0])] + [apart(b) for b in up[1]]
    arrays += [apart(b) for b in qkv[0]] + [apart(b) for b in qkv[1]]
    return pl.pallas_call(
        functools.partial(weight_kernel, micro),
        in_specs=[pl.BlockSpec(memory_space=pltpu.SMEM)] + [free] * len(arrays),
        out_shape=[jax.ShapeDtypeStruct((256, part), BF16)] * (2 * PARTS),
        scratch_shapes=[
            pltpu.VMEM((2 * tokens, 512), BF16),
            pltpu.VMEM((2 * tokens, 512), BF16),
            pltpu.VMEM((2 * tokens, wide), BF16),
            pltpu.VMEM((2 * tokens, narrow), BF16),
            pltpu.VMEM((512, 2 * tokens), BF16),
            pltpu.SemaphoreType.DMA((10 + 10 * micro,)),
        ],
        compiler_params=pltpu.CompilerParams(vmem_limit_bytes=32 << 20),
        cost_estimate=pl.CostEstimate(flops=8 * tokens * 512 * 2 * half, bytes_accessed=9 << 20, transcendentals=0),
        name="weight_parts",
    )(blocks, *arrays)


def added(a, b):
    return (a.astype(F32) + b.astype(F32)).astype(BF16)


def weight_sums(normed, up, qkv, attn):
    y, z, c = fsdp_place(lax.axis_index("fsdp"))

    def parts(*moves):
        bases = [2 * ((z + dz) % DEPTH) + c for dz in moves]
        return weight_parts(
            jnp.stack([base + 2 * DEPTH * i for base in bases for i in range(2)]), normed, up, qkv, attn
        )

    before, after = (lambda got: (got[:PARTS], got[PARTS:]))(parts(-1, 1))
    way = [1] * (PARTS // 2) + [-1] * (PARTS // 2)
    one = [before[k] if way[k] == 1 else after[k] for k in range(PARTS)]
    three = [after[k] if way[k] == 1 else before[k] for k in range(PARTS)]
    order = [k + h for k in range(PARTS // 2) for h in (0, PARTS // 2)]
    sums = {k: fsdp_move(one[k], 0, way[k], 0) for k in order}
    two, last = (lambda got: (got[:PARTS], got[PARTS:]))(parts(2, 0))
    for term in (two, three):
        sums = {k: fsdp_move(added(sums[k], term[k]), 0, way[k], 0) for k in order}

    def rows(block, which):
        return jnp.where(which == 0, block[:128], block[128:]).astype(F32)

    result = {}
    for k in range(PARTS // 2):
        pair = (k, k + PARTS // 2)
        there = jnp.concatenate([(rows(sums[h], 1 - y) + rows(last[h], 1 - y)).astype(BF16) for h in pair], axis=1)
        there = fsdp_move(there, 1, 0, 0)
        width = there.shape[1] // 2
        for i, h in enumerate(pair):
            here = rows(sums[h], y) + rows(last[h], y)
            result[h] = (here + there[:, i * width : (i + 1) * width].astype(F32)).astype(BF16)
    return jnp.concatenate([result[k] for k in range(PARTS)], axis=1)


def shard_kernel(wq_ref, wk_ref, wv_ref, wo_ref, out_ref):
    place = 0
    for ref in (wq_ref, wk_ref, wv_ref):
        for start in range(0, ref.shape[1], 128):
            out_ref[place : place + 128] = ref[:, start : start + 128].astype(F32).T.astype(BF16)
            place += 128
    for start in range(0, wo_ref.shape[1], 128):
        out_ref[place : place + 128] = wo_ref[:, start : start + 128]
        place += 128


def shard_blocks(*weights):
    total = sum(b.shape[1] for b in weights)
    return pl.pallas_call(
        shard_kernel,
        out_shape=jax.ShapeDtypeStruct((total, weights[0].shape[0]), BF16),
        compiler_params=pltpu.CompilerParams(vmem_limit_bytes=8 << 20),
        name="shard_blocks",
    )(*[pltpu.with_memory_space_constraint(b, pltpu.HBM) for b in weights])


def gathered(shard, qkv, first, second):
    across = lambda b: fsdp_move(b, 0, 0, 1)
    other, below, above = fsdp_move(shard, 1, 0, 0), fsdp_move(shard, 0, 1, 0), fsdp_move(shard, 0, -1, 0)
    own_swap = across(shard)
    other, below, above, own_swap, first = lax.optimization_barrier((other, below, above, own_swap, first))
    other_below, other_above = fsdp_move(other, 0, 1, 0), fsdp_move(other, 0, -1, 0)
    far_in, far_out = fsdp_move(below[:qkv], 0, 1, 0), fsdp_move(above[qkv:], 0, -1, 0)
    beside = second(*first)
    other_below, other_above, far_in, far_out, beside = lax.optimization_barrier(
        (other_below, other_above, far_in, far_out, beside)
    )
    next_in, next_out = other_below[:qkv], other_above[qkv:]
    last_in, last_out = fsdp_move(next_in, 0, 1, 0), fsdp_move(next_out, 0, -1, 0)
    below, above, other, far_in, far_out, _ = lax.optimization_barrier(
        (below, above, other, far_in, far_out, (next_in, next_out))
    )
    arrays = [shard, below, above, other, other_below, other_above, far_in, far_out, last_in, last_out]
    moves = [(0, 0), (0, -1), (0, 1), (1, 0), (1, -1), (1, 1), (0, 2), (0, 2), (1, 2), (1, 2)]
    parts = [None] * 6 + [0, 1, 0, 1]
    places = [
        (k + dc * len(arrays), 0, part, (*move, dc)) for dc in range(2) for k, (part, move) in enumerate(zip(parts, moves))
    ]
    return arrays + [own_swap] + [across(b) for b in arrays[1:]], places, beside


def arrange_kernel(places, place_ref, *refs):
    count = 1 + max(k for k, _, _, _ in places)
    pieces, (wo_ref, wi_ref), sem = refs[:count], refs[count : count + 2], refs[-1]
    qkv = wi_ref.shape[0]
    copies = []
    for i, (k, row, part, _) in enumerate(places):
        own = pl.ds(pl.multiple_of(place_ref[i] * 128, 128), 128)
        if part != 1:
            copies.append(pltpu.make_async_copy(pieces[k].at[pl.ds(row, qkv)], wi_ref.at[:, own], sem))
            row += qkv
        if part != 0:
            for b in range(wo_ref.shape[1] // 128):
                block = pieces[k].at[pl.ds(row + b * 128, 128)]
                copies.append(pltpu.make_async_copy(block, wo_ref.at[own, pl.ds(b * 128, 128)], sem))
    for copy in copies:
        copy.start()
    for copy in copies:
        copy.wait()


def arrange(arrays, places, micro, length, width, qd, qkv):
    y, z, c = fsdp_place(lax.axis_index("fsdp"))
    place = jnp.stack(
        [(((y + dy) % 2) * DEPTH + (z + dz) % DEPTH) * 2 + (c + dc) % 2 for _, _, _, (dy, dz, dc) in places]
    )
    hbm = pl.BlockSpec(memory_space=pltpu.HBM)
    free = pl.BlockSpec(memory_space=pl.ANY)
    vmem = pl.BlockSpec(memory_space=pltpu.VMEM)
    rows = [pltpu.HBM((length, qkv), BF16)] * micro + [pltpu.HBM((length, width), BF16)] * micro
    wo, wi, acc, arrived, act, *rest = pl.pallas_call(
        functools.partial(arrange_kernel, places),
        in_specs=[pl.BlockSpec(memory_space=pltpu.SMEM)] + [free] * len(arrays),
        out_specs=[vmem, vmem, vmem, vmem, hbm] + [hbm] * len(rows),
        out_shape=[
            pltpu.VMEM((width, qd), BF16),
            pltpu.VMEM((qkv, width), BF16),
            pltpu.VMEM((2 * KVH * HD, length), F32),
            pltpu.VMEM((ROWS, width), BF16),
            pltpu.HBM((micro, length, width), BF16),
            *rows,
        ],
        scratch_shapes=[pltpu.SemaphoreType.DMA],
        compiler_params=pltpu.CompilerParams(vmem_limit_bytes=40 << 20),
        name="arrange",
    )(place, *[pltpu.with_memory_space_constraint(b, pltpu.HBM) for b in arrays])
    return wo, wi, acc, arrived, act, rest[:micro], rest[micro:]


def paired(blocks):
    turned = blocks.transpose(0, 2, 3, 1)
    zero = jnp.zeros_like(turned)
    return jnp.concatenate(
        [jnp.concatenate([turned, zero], axis=3), jnp.concatenate([zero, turned], axis=3)], axis=2
    )


def on_device(x, q, k, v, cot, gain, wq, wk, wv, wo):
    sections = lax.axis_size("section")
    me = lax.axis_index("section")
    x, q, k, v, gain = x[0], q[0], k[0], v[0], gain
    micro, length, width = x.shape
    chunks = length // ROWS
    qd, kvd = HEADS * HD, KVH * HD
    shard = shard_blocks(wq[0], wk[0], wv[0], wo[0])
    turns = sections - 1 + chunks
    step = jnp.arange(turns, dtype=jnp.int32) - (sections - 1 - me)
    place = jnp.stack(
        [
            chunks - 1 - jnp.clip(step, 0, chunks - 1),
            ((step >= 0) & (step < chunks)).astype(jnp.int32),
            jnp.broadcast_to((me == sections - 1).astype(jnp.int32), (turns,)),
            (step <= 0).astype(jnp.int32),
        ],
        axis=1,
    ).reshape(-1)
    kh = k.reshape(micro, length, KVH, HD)
    vh = v.reshape(micro, length, KVH, HD)
    kg = kh.transpose(0, 2, 1, 3)
    vg = vh.transpose(0, 2, 1, 3)
    cos, sin = rotary_tables(length)
    swapped_keys = jnp.concatenate([kg[..., HD // 2 :], kg[..., : HD // 2]], axis=-1)
    kcat = jnp.concatenate([kg, swapped_keys], axis=-1)
    tables = (jnp.concatenate([cos, cos, sin, -sin], axis=1), cos.T, sin.T)

    def forward(q, kbd, vdup, vbd, kcat, tables, place):
        normed, p, attn, qt = forward_parts(x, q, kbd, vdup, gain)
        normed, attn = [b.reshape(micro * length, -1) for b in (normed, attn)]
        return normed, p, attn, qt, vbd, kcat, tables, place

    arrays, places, beside = gathered(
        shard,
        qd + 2 * kvd,
        (q, paired(kh), jnp.concatenate([vg, vg], axis=-1), paired(vh), kcat, tables, place),
        forward,
    )
    normed, p, attn, qt, vbd, kcat, (cs, ct, st), place = beside
    normed_both, attn_both = (normed, fsdp_move(normed, 0, 0, 1)), (attn, fsdp_move(attn, 0, 0, 1))
    arrays, normed_both, attn_both = lax.optimization_barrier((arrays, normed_both, attn_both))
    wo, wi, acc, arrived, act, qkv, up = arrange(arrays, places, micro, length, width, qd, qd + 2 * kvd)
    acc, arrived = [acc] * micro, [arrived] * micro
    sent = list(arrived)
    for turn in range(turns):
        for m in range(micro):
            sent[m], acc[m], act, qkv[m], up[m] = turn_step(
                m, turn, turn == turns - 1, place, arrived[m], sent[m], cot, x, p, qt, kcat, vbd, gain, cs, ct, st, wo, wi,
                acc[m], act, qkv[m], up[m],
            )
            if turn < turns - 1:
                arrived[m] = passed_down(sent[m])
    swapped = [[fsdp_move(b, 0, 0, 1) for b in (up[m], qkv[m])] for m in range(micro)]
    ups, qkvs = [[[own[m] for m in range(micro)], [swapped[m][k] for m in range(micro)]] for k, own in enumerate((up, qkv))]
    summed = weight_sums(normed_both, ups, qkvs, attn_both)
    return (
        act[None],
        summed[None, :, :qd],
        summed[None, :, qd : qd + kvd],
        summed[None, :, qd + kvd : qd + 2 * kvd],
        summed[None, :, qd + 2 * kvd :],
    )


def solution(mesh):
    row = P("section", None, "fsdp", None)
    weight = P("section", "fsdp", None)
    return jax.shard_map(
        on_device,
        mesh=mesh,
        in_specs=(row, row, row, row, P(None, "fsdp", None), P("section", None), weight, weight, weight, weight),
        out_specs=(row, weight, weight, weight, weight),
        check_vma=False,
    )
```
